512 devices in a mesh: dp: 32 (over x, y), tensor: 16 (over z, core).
Axes of the slice: x: 4, y: 8, z: 8, core: 2. Of those that a mesh axis runs over, the one named last changes fastest.
Arguments:
- queries: bfloat16 [128, 4, 128, 128], P('dp', None, 'tensor'), parts along dimension 0, may hold values from -18 to 18
- cache: bfloat16 [16, 128, 256, 256], P('tensor', 'dp'), parts along dimension 1, may hold values from -10 to 10
- new_kv: bfloat16 [16, 128, 4, 256], P('tensor', 'dp'), parts along dimension 1, may hold values from -6 to 6
- cache_len: int32 [128], P('dp'), parts along dimension 0, may hold values from 64 to 256, as said below
- target_logits: bfloat16 [512, 128256], P('dp', 'tensor'), parts along dimension 0, may hold values from -19 to 262
- drafter: bfloat16 [512, 2, 16, 8016], P(('dp', 'tensor')), parts along dimension 0, may hold values from 0.0009 to 3.01, as said below
- draft_tokens: int32 [512], P('dp'), parts along dimension 0, may hold values from 0 to 128255
- language: int32 [128], P('dp'), parts along dimension 0, may hold values from 0 to 1
- uniforms: float32 [512], P('dp'), parts along dimension 0, may hold values from 0 to 1
Outputs:
- attn_out: bfloat16 [128, 4, 128, 128], P('dp', None, 'tensor'), parts along dimension 0
- accept_margin: float32 [512], P('dp'), parts along dimension 0
- residual_mass: float32 [512], P('dp'), parts along dimension 0
The draws below stay inside these ranges and needn't reach their ends.
There are 32 independent parts, one for each index of `dp`. The reference program is written for one: setup_inputs(seed, part) draws one part's arguments, and reference() takes and returns one part's arrays. A program takes and returns all parts, laid end to end along the dimension named above; each array names one. Nothing has to cross between parts.
Inputs may be any that keep to these rules, and one draw needn't show every extreme that they name: `cache_len`: every request has 64 or more positions in use; some request has exactly 256. `drafter`: entries are positive.
All inputs are finite; a program needn't handle non-finite values.
Results may differ from the reference program's by a relative error of at most 0.0049.
Values may be sent and summed in bfloat16 or wider, within the bound.
A program may use at most 64 MiB of HBM per device.

```python
import math
import jax
import jax.numpy as jnp
from jax import lax

HEADS = 128
HEAD_DIM = 128
VOCAB = 128256
DRAFTS = 4
LANGS = 2
ROWS = 4
CACHE = 256
SLOTS = 16
KV_SLOTS = 16
VSHARD = 8016


def peak_mask(key):
    share = max(160.0 / VOCAB, 0.04)
    return jax.random.bernoulli(jax.random.fold_in(key, 90), share, (SLOTS, VOCAB))


def draw_queries(key, part):
    base = jnp.clip(jax.random.normal(jax.random.fold_in(key, 1), (ROWS, DRAFTS, HEADS, HEAD_DIM), jnp.float32), -6.0, 6.0)
    return base.astype(jnp.bfloat16)


def draw_cache(key, part):
    cache_keys = jnp.clip(jax.random.normal(jax.random.fold_in(key, 4), (KV_SLOTS, ROWS, CACHE, HEAD_DIM), jnp.float32), -6.0, 6.0)
    cache_values = jnp.clip(jax.random.normal(jax.random.fold_in(key, 5), (KV_SLOTS, ROWS, CACHE, HEAD_DIM), jnp.float32), -6.0, 6.0)
    return jnp.concatenate([cache_keys, cache_values], axis=3).astype(jnp.bfloat16)


def draw_cache_len(key, part):
    lengths = jax.random.randint(jax.random.fold_in(key, 21), (ROWS,), CACHE // 4, CACHE + 1)
    longest = jax.random.randint(jax.random.fold_in(key, 22), (), 0, ROWS)
    return jnp.where(jnp.arange(ROWS) == longest, CACHE, lengths).astype(jnp.int32)


def draw_target_logits(key, part):
    peaks = peak_mask(key)
    noise = jnp.clip(jax.random.normal(jax.random.fold_in(key, 31), (SLOTS, VOCAB), jnp.float32), -6.0, 6.0)
    ramp = 1.1 * jnp.arange(VOCAB, dtype=jnp.float32)[None, :] / VOCAB
    logits = jnp.where(peaks, 12.0 + noise, 3.0 * noise) + ramp
    return logits.astype(jnp.bfloat16)


def draw_drafter(key, part):
    peaks = peak_mask(key)[:, None, :]
    ramp = 1.0 + 2.0 * jnp.arange(VOCAB, dtype=jnp.float32)[None, None, :] / VOCAB
    exponent = jax.random.uniform(jax.random.fold_in(key, 42), (SLOTS, LANGS, VOCAB), jnp.float32, jnp.log(0.001), jnp.log(0.01))
    height = jax.random.uniform(jax.random.fold_in(key, 44), (SLOTS, LANGS, VOCAB), jnp.float32, 0.6, 1.0)
    values = jnp.where(peaks, height, jnp.exp(exponent)) * ramp
    return values.reshape(SLOTS, LANGS, VOCAB // VSHARD, VSHARD).astype(jnp.bfloat16)


def plant(result, key, least, high):
    longest = result.shape.index(max(result.shape))
    spots = []
    for shift in (0, 1):
        where = [jax.random.randint(jax.random.fold_in(key, axis), (), 0, length) for axis, length in enumerate(result.shape)]
        where[longest] = (where[longest] + shift) % result.shape[longest]
        spots.append(tuple(where))
    return result.at[spots[0]].set(least).at[spots[1]].set(high)


def levels(own_key, shape, pieces, low, top_value):
    level, own = 1.0, jax.random.fold_in(own_key, 6)
    for axis_at, shards_of in pieces:
        steps = jnp.exp(jax.random.uniform(jax.random.fold_in(own, axis_at), (shards_of,), jnp.float32, low / len(pieces), top_value / len(pieces)))
        level = level * jnp.repeat(steps, shape[axis_at] // shards_of).reshape([-1 if axis == axis_at else 1 for axis in range(len(shape))])
    return level


def normal_values(key, extent, deviation, most, pieces=(), kind=jnp.bfloat16):
    drawn = jax.random.normal(key, extent, jnp.float32) * deviation
    if len(pieces) > 0:
        drawn = levels(key, extent, pieces, -0.22, 0.18) * drawn
    return jnp.clip(drawn, min=-most, max=most).astype(kind)


def setup_inputs(seed: int = 0, part: int = 0) -> dict:
    splits = jax.random.split(jax.random.key(seed), 10)
    own_keys = jax.random.split(jax.random.fold_in(splits[9], part), 10)
    queries = draw_queries(jax.random.fold_in(jax.random.fold_in(splits[9], part), 71), part)
    cache = draw_cache(jax.random.fold_in(jax.random.fold_in(splits[9], part), 71), part)
    new_kv = normal_values(own_keys[2], (KV_SLOTS, ROWS, DRAFTS, 2 * HEAD_DIM), 1.0, 6.0, ((0, 16),))
    cache_len = draw_cache_len(jax.random.fold_in(jax.random.fold_in(splits[9], part), 71), part)
    target_logits = draw_target_logits(jax.random.fold_in(jax.random.fold_in(splits[9], part), 71), part)
    drafter = draw_drafter(jax.random.fold_in(jax.random.fold_in(splits[9], part), 71), part)
    draft_tokens = plant(jax.random.randint(own_keys[6], (SLOTS,), 0, VOCAB), jax.random.fold_in(own_keys[6], 1), 0, VOCAB - 1).astype(jnp.int32)
    language = plant(jax.random.randint(own_keys[7], (ROWS,), 0, LANGS), jax.random.fold_in(own_keys[7], 1), 0, LANGS - 1).astype(jnp.int32)
    uniforms = jnp.clip(jax.random.uniform(own_keys[8], (SLOTS,), jnp.float32, 0.0, 1.0), 0.0, 1.0)
    return {"queries": queries, "cache": cache, "new_kv": new_kv, "cache_len": cache_len, "target_logits": target_logits, "drafter": drafter, "draft_tokens": draft_tokens, "language": language, "uniforms": uniforms}


def reference(queries, cache, new_kv, cache_len, target_logits, drafter, draft_tokens, language, uniforms):
    group_size = HEADS // KV_SLOTS
    query_f = queries.astype(jnp.float32).reshape(ROWS, DRAFTS, KV_SLOTS, group_size, HEAD_DIM)
    all_keys = jnp.concatenate([cache[..., :HEAD_DIM], new_kv[..., :HEAD_DIM]], axis=2).astype(jnp.float32)
    all_values = jnp.concatenate([cache[..., HEAD_DIM:], new_kv[..., HEAD_DIM:]], axis=2).astype(jnp.float32)
    scores = jnp.einsum('rigkd,grtd->rgikt', query_f, all_keys) * (1.0 / math.sqrt(HEAD_DIM))
    position = jnp.arange(CACHE + DRAFTS)
    past_ok = (position[None, :] < cache_len[:, None]) & (position[None, :] < CACHE)
    fresh_index = position - CACHE
    fresh_ok = (fresh_index[None, :] >= 0) & (fresh_index[None, :] <= jnp.arange(DRAFTS)[:, None])
    allowed = past_ok[:, None, None, None, :] | fresh_ok[None, None, :, None, :]
    scores = jnp.where(allowed, scores, -jnp.inf)
    row_peak = lax.optimization_barrier(jnp.max(scores, axis=-1, keepdims=True))
    exp_terms = jnp.exp(scores - row_peak)
    weights = (exp_terms / lax.optimization_barrier(jnp.sum(exp_terms, axis=-1, keepdims=True))).astype(jnp.bfloat16)
    mixed = jnp.einsum('rgikt,grtd->rigkd', weights.astype(jnp.float32), all_values)
    attn_out = mixed.reshape(ROWS, DRAFTS, HEADS, HEAD_DIM).astype(jnp.bfloat16)
    logits = target_logits.astype(jnp.float32)
    logit_peak = lax.optimization_barrier(jnp.max(logits, axis=1, keepdims=True))
    logit_exp = jnp.exp(logits - logit_peak)
    target_probs = logit_exp / lax.optimization_barrier(jnp.sum(logit_exp, axis=1, keepdims=True))
    slot_lang = jnp.repeat(language, DRAFTS)
    flat_drafter = drafter.reshape(SLOTS, LANGS, VOCAB)
    chosen = flat_drafter[:, 0]
    for lang_index in range(1, LANGS):
        chosen = jnp.where(slot_lang[:, None] == lang_index, flat_drafter[:, lang_index], chosen)
    draft_weights = chosen.astype(jnp.float32)
    drafted = draft_weights / lax.optimization_barrier(jnp.sum(draft_weights, axis=1, keepdims=True))
    marked = jnp.arange(VOCAB)[None, :] == draft_tokens[:, None]
    draft_prob = lax.optimization_barrier(jnp.sum(jnp.where(marked, target_probs, 0.0), axis=1))
    draft_share = lax.optimization_barrier(jnp.sum(jnp.where(marked, drafted, 0.0), axis=1))
    accept_margin = jnp.minimum(1.0, draft_prob / draft_share) - uniforms
    residual_mass = lax.optimization_barrier(jnp.sum(jnp.maximum(target_probs - drafted, 0.0), axis=1))
    return (attn_out, accept_margin, residual_mass)
```

```python
import math

import jax
import jax.numpy as jnp
from jax import lax
from jax.experimental import pallas as pl
from jax.experimental.pallas import tpu as pltpu
from jax.sharding import PartitionSpec as P

MESH = pl.DeviceIdType.MESH
GROUP = 16
LANES = 128
VSHARD = 8016
FULL = VSHARD // LANES
TAIL = VSHARD - FULL * LANES
CHUNKS = 64
ABSENT = -3.0e38
ORDER = (8, 9, 7, 10, 6, 11, 5, 12, 4, 13, 3, 14, 2, 15, 1)


def spread(load, tiles, fill):
    for c in range(FULL):
        tiles[pl.ds(GROUP * c, GROUP), :] = load(c * LANES, LANES).astype(jnp.float32)
    rest = (CHUNKS - FULL) * GROUP
    tiles[pl.ds(GROUP * FULL, rest), :] = jnp.full((rest, LANES), fill, jnp.float32)
    tiles[pl.ds(GROUP * FULL, GROUP), 0:TAIL] = load(FULL * LANES, TAIL).astype(jnp.float32)


def attend(r, q, kv, fresh, used):
    depth = q.shape[-1]
    scale = 1.0 / math.sqrt(depth)
    query = q[r].astype(jnp.float32).reshape(32, depth).astype(jnp.bfloat16)
    nt = (((1,), (1,)), ((), ()))
    nn = (((1,), (0,)), ((), ()))
    past = kv[0, r]
    new = fresh[0, r]
    past_scores = (
        lax.dot_general(query, past[:, :depth], nt, preferred_element_type=jnp.float32) * scale
    )
    new_scores = (
        lax.dot_general(query, new[:, :depth], nt, preferred_element_type=jnp.float32) * scale
    )
    position = lax.broadcasted_iota(jnp.int32, past_scores.shape, 1)
    past_scores = jnp.where(position < used, past_scores, -jnp.inf)
    draft = lax.broadcasted_iota(jnp.int32, new_scores.shape, 0) // 8
    key = lax.broadcasted_iota(jnp.int32, new_scores.shape, 1)
    new_scores = jnp.where(key <= draft, new_scores, -jnp.inf)
    peak = jnp.maximum(
        jnp.max(past_scores, axis=1, keepdims=True), jnp.max(new_scores, axis=1, keepdims=True)
    )
    past_exp = jnp.exp(past_scores - peak)
    new_exp = jnp.exp(new_scores - peak)
    total = jnp.sum(past_exp, axis=1, keepdims=True) + jnp.sum(new_exp, axis=1, keepdims=True)
    past_w = (past_exp / total).astype(jnp.bfloat16)
    new_w = (new_exp / total).astype(jnp.bfloat16)
    mixed = lax.dot_general(past_w, past[:, depth:], nn, preferred_element_type=jnp.float32)
    mixed = mixed + lax.dot_general(new_w, new[:, depth:], nn, preferred_element_type=jnp.float32)
    return mixed.reshape(4, 8, depth).astype(jnp.bfloat16)


def kernel(
    q_in,
    kv_in,
    fresh_in,
    used_in,
    logits_in,
    drafter_in,
    token_in,
    language_in,
    uniform_in,
    attn_out,
    margin_out,
    mass_out,
    q,
    kv,
    fresh,
    logits,
    drafter,
    used,
    token,
    language,
    uniform,
    tiles,
    shares,
    send,
    arrived,
    terms,
    peaks,
    stat,
    stats,
    load_sem,
    send_sem,
    recv_sem,
    stat_send,
    stat_recv,
):
    me = lax.axis_index("tensor")
    barrier = pltpu.get_barrier_semaphore()
    for k in ORDER:
        peer = lax.rem(me + k, GROUP)
        pl.semaphore_signal(barrier, inc=1, device_id={"tensor": peer}, device_id_type=MESH)

    loads = []
    for at, (src, dst) in enumerate(
        (
            (logits_in, logits),
            (language_in, language),
            (drafter_in, drafter),
            (token_in, token),
            (uniform_in, uniform),
            (used_in, used),
            (q_in, q),
            (kv_in, kv),
            (fresh_in, fresh),
        )
    ):
        copy = pltpu.make_async_copy(src, dst, load_sem.at[at])
        copy.start()
        loads.append(copy)

    loads[0].wait()
    spread(lambda at, n: logits[:, at : at + n], tiles, ABSENT)
    for s in range(GROUP):
        send[s] = tiles[pl.ds(s, CHUNKS, stride=GROUP), :].astype(jnp.bfloat16)
    pl.semaphore_wait(barrier, GROUP - 1)
    copies = {}
    for k in ORDER:
        peer = lax.rem(me + k, GROUP)
        copy = pltpu.make_async_remote_copy(
            src_ref=send.at[peer],
            dst_ref=arrived.at[k],
            send_sem=send_sem.at[k],
            recv_sem=recv_sem.at[k],
            device_id={"tensor": peer},
            device_id_type=MESH,
        )
        copy.start()
        copies[k] = copy
    arrived[0] = send[me]

    for copy in loads[1:]:
        copy.wait()
    lang = language[me // 4]
    spread(lambda at, n: drafter[0, lang, :, at : at + n], shares, 0.0)
    total = jnp.sum(shares[...].reshape(CHUNKS * GROUP // 8, 8, LANES), axis=0)
    total = jnp.sum(total, axis=(0, 1), keepdims=True)
    inverse = 1.0 / total

    for r in range(4):
        attn_out[r] = attend(r, q, kv, fresh, used[r])

    place = lax.broadcasted_iota(jnp.int32, (CHUNKS, LANES), 0) * LANES + lax.broadcasted_iota(
        jnp.int32, (CHUNKS, LANES), 1
    )
    wanted = token[me]
    for k in (0,) + ORDER[::-1]:
        if k:
            copies[k].wait_recv()
        block = arrived[k].astype(jnp.float32).reshape(8, 8, LANES)
        peak = jnp.max(block, axis=0)
        peaks[k] = peak
        terms[k] = jnp.exp(block - peak[None])

    top = jnp.max(peaks[...], axis=0)
    top = jnp.max(top, axis=(0, 1), keepdims=True)
    norm = jnp.zeros((8, LANES), jnp.float32)
    for k in range(GROUP):
        norm = norm + jnp.sum(terms[k], axis=0) * jnp.exp(peaks[k] - top)
    norm = jnp.sum(norm, axis=(0, 1), keepdims=True)
    mass = jnp.zeros((8, LANES), jnp.float32)
    prob = jnp.zeros((8, LANES), jnp.float32)
    share = jnp.zeros((8, LANES), jnp.float32)
    for k in range(GROUP):
        piece = lax.rem(me + GROUP - k, GROUP)
        probs = terms[k] * (jnp.exp(peaks[k] - top) / norm)[None]
        drafted = shares[pl.ds(piece, CHUNKS, stride=GROUP), :].reshape(8, 8, LANES) * inverse[None]
        mass = mass + jnp.sum(jnp.maximum(probs - drafted, 0.0), axis=0)
        hit = (place == wanted - piece * VSHARD).reshape(8, 8, LANES)
        prob = prob + jnp.sum(jnp.where(hit, probs, 0.0), axis=0)
        share = share + jnp.sum(jnp.where(hit, drafted, 0.0), axis=0)
    mass = jnp.sum(mass, axis=(0, 1), keepdims=True)
    prob = jnp.sum(prob, axis=(0, 1), keepdims=True)
    share = jnp.sum(share, axis=(0, 1), keepdims=True)
    margin = jnp.minimum(1.0, prob / share) - uniform[me]

    lane = lax.broadcasted_iota(jnp.int32, (1, LANES), 1)
    row = jnp.where(lane == me, margin, 0.0) + jnp.where(lane == me + GROUP, mass, 0.0)
    stat[...] = row
    stat_copies = []
    for k in ORDER:
        peer = lax.rem(me + k, GROUP)
        copy = pltpu.make_async_remote_copy(
            src_ref=stat,
            dst_ref=stats.at[k - 1],
            send_sem=stat_send.at[k],
            recv_sem=stat_recv.at[k],
            device_id={"tensor": peer},
            device_id_type=MESH,
        )
        copy.start()
        stat_copies.append(copy)
    for k in ORDER:
        copies[k].wait_send()
    for copy in stat_copies:
        copy.wait()
    row = row + jnp.sum(stats[...], axis=0)
    margin_out[...] = row[0, 0:GROUP]
    mass_out[...] = row[0, GROUP : 2 * GROUP]


def on_device(
    queries, cache, new_kv, cache_len, target_logits, drafter, draft_tokens, language, uniforms
):
    anywhere = pl.BlockSpec(memory_space=pltpu.HBM)
    vmem = pl.BlockSpec(memory_space=pltpu.VMEM)
    f32 = jnp.float32
    bf16 = jnp.bfloat16
    return pl.pallas_call(
        kernel,
        out_shape=(
            jax.ShapeDtypeStruct(queries.shape, bf16),
            jax.ShapeDtypeStruct((GROUP,), f32),
            jax.ShapeDtypeStruct((GROUP,), f32),
        ),
        in_specs=[anywhere] * 9,
        out_specs=(vmem, vmem, vmem),
        scratch_shapes=[
            pltpu.VMEM(queries.shape, bf16),
            pltpu.VMEM(cache.shape, bf16),
            pltpu.VMEM(new_kv.shape, bf16),
            pltpu.VMEM(target_logits.shape, bf16),
            pltpu.VMEM(drafter.shape, bf16),
            pltpu.SMEM(cache_len.shape, jnp.int32),
            pltpu.SMEM(draft_tokens.shape, jnp.int32),
            pltpu.SMEM(language.shape, jnp.int32),
            pltpu.SMEM(uniforms.shape, f32),
            pltpu.VMEM((CHUNKS * GROUP, LANES), f32),
            pltpu.VMEM((CHUNKS * GROUP, LANES), f32),
            pltpu.VMEM((GROUP, CHUNKS, LANES), bf16),
            pltpu.VMEM((GROUP, CHUNKS, LANES), bf16),
            pltpu.VMEM((GROUP, 8, 8, LANES), f32),
            pltpu.VMEM((GROUP, 8, LANES), f32),
            pltpu.VMEM((1, LANES), f32),
            pltpu.VMEM((GROUP - 1, 1, LANES), f32),
            pltpu.SemaphoreType.DMA((9,)),
            pltpu.SemaphoreType.DMA((GROUP,)),
            pltpu.SemaphoreType.DMA((GROUP,)),
            pltpu.SemaphoreType.DMA((GROUP,)),
            pltpu.SemaphoreType.DMA((GROUP,)),
        ],
        compiler_params=pltpu.CompilerParams(
            collective_id=0, has_side_effects=True, vmem_limit_bytes=32 * 1024 * 1024
        ),
    )(queries, cache, new_kv, cache_len, target_logits, drafter, draft_tokens, language, uniforms)


def solution(mesh):
    in_specs = (
        P("dp", None, "tensor", None),
        P("tensor", "dp", None, None),
        P("tensor", "dp", None, None),
        P("dp"),
        P("dp", "tensor"),
        P(("dp", "tensor"), None, None, None),
        P("dp"),
        P("dp"),
        P("dp"),
    )
    out_specs = (P("dp", None, "tensor", None), P("dp"), P("dp"))
    return jax.shard_map(
        on_device, mesh=mesh, in_specs=in_specs, out_specs=out_specs, check_vma=False
    )
```

```python
import math

import jax
import jax.numpy as jnp
from jax import lax
from jax.experimental import pallas as pl
from jax.experimental.pallas import tpu as pltpu
from jax.sharding import PartitionSpec as P

MESH = pl.DeviceIdType.MESH
GROUP = 16
LANES = 128
VSHARD = 8016
FULL = VSHARD // LANES
TAIL = VSHARD - FULL * LANES
CHUNKS = 64
ABSENT = -3.0e38
ORDER = (8, 9, 7, 10, 6, 11, 5, 12, 4, 13, 3, 14, 2, 15, 1)


def spread(load, tiles, fill):
    for c in range(FULL):
        tiles[pl.ds(GROUP * c, GROUP), :] = load(c * LANES, LANES).astype(jnp.float32)
    rest = (CHUNKS - FULL) * GROUP
    tiles[pl.ds(GROUP * FULL, rest), :] = jnp.full((rest, LANES), fill, jnp.float32)
    tiles[pl.ds(GROUP * FULL, GROUP), 0:TAIL] = load(FULL * LANES, TAIL).astype(jnp.float32)


def attend(r, q, kv, fresh, used):
    depth = q.shape[-1]
    scale = 1.0 / math.sqrt(depth)
    query = q[r].astype(jnp.float32).reshape(32, depth).astype(jnp.bfloat16)
    nt = (((1,), (1,)), ((), ()))
    nn = (((1,), (0,)), ((), ()))
    past = kv[0, r]
    new = fresh[0, r]
    past_scores = (
        lax.dot_general(query, past[:, :depth], nt, preferred_element_type=jnp.float32) * scale
    )
    new_scores = (
        lax.dot_general(query, new[:, :depth], nt, preferred_element_type=jnp.float32) * scale
    )
    position = lax.broadcasted_iota(jnp.int32, past_scores.shape, 1)
    past_scores = jnp.where(position < used, past_scores, -jnp.inf)
    draft = lax.broadcasted_iota(jnp.int32, new_scores.shape, 0) // 8
    key = lax.broadcasted_iota(jnp.int32, new_scores.shape, 1)
    new_scores = jnp.where(key <= draft, new_scores, -jnp.inf)
    peak = jnp.maximum(
        jnp.max(past_scores, axis=1, keepdims=True), jnp.max(new_scores, axis=1, keepdims=True)
    )
    past_exp = jnp.exp(past_scores - peak)
    new_exp = jnp.exp(new_scores - peak)
    total = jnp.sum(past_exp, axis=1, keepdims=True) + jnp.sum(new_exp, axis=1, keepdims=True)
    past_w = (past_exp / total).astype(jnp.bfloat16)
    new_w = (new_exp / total).astype(jnp.bfloat16)
    mixed = lax.dot_general(past_w, past[:, depth:], nn, preferred_element_type=jnp.float32)
    mixed = mixed + lax.dot_general(new_w, new[:, depth:], nn, preferred_element_type=jnp.float32)
    return mixed.reshape(4, 8, depth).astype(jnp.bfloat16)


def kernel(
    q_in,
    kv_in,
    fresh_in,
    used_in,
    logits_in,
    drafter_in,
    token_in,
    language_in,
    uniform_in,
    attn_out,
    margin_out,
    mass_out,
    q,
    kv,
    fresh,
    logits,
    drafter,
    used,
    token,
    language,
    uniform,
    tiles,
    shares,
    send,
    arrived,
    terms,
    peaks,
    stat,
    stats,
    load_sem,
    send_sem,
    recv_sem,
    stat_send,
    stat_recv,
):
    me = lax.axis_index("tensor")
    barrier = pltpu.get_barrier_semaphore()
    for k in ORDER:
        peer = lax.rem(me + k, GROUP)
        pl.semaphore_signal(barrier, inc=1, device_id={"tensor": peer}, device_id_type=MESH)

    loads = []
    for at, (src, dst) in enumerate(
        (
            (logits_in, logits),
            (language_in, language),
            (drafter_in, drafter),
            (token_in, token),
            (uniform_in, uniform),
            (used_in, used),
            (q_in, q),
            (kv_in, kv),
            (fresh_in, fresh),
        )
    ):
        copy = pltpu.make_async_copy(src, dst, load_sem.at[at])
        copy.start()
        loads.append(copy)

    loads[0].wait()
    spread(lambda at, n: logits[:, at : at + n], tiles, ABSENT)
    for s in range(GROUP):
        send[s] = tiles[pl.ds(s, CHUNKS, stride=GROUP), :].astype(jnp.bfloat16)
    pl.semaphore_wait(barrier, GROUP - 1)
    copies = {}
    for k in ORDER:
        peer = lax.rem(me + k, GROUP)
        copy = pltpu.make_async_remote_copy(
            src_ref=send.at[peer],
            dst_ref=arrived.at[k],
            send_sem=send_sem.at[k],
            recv_sem=recv_sem.at[k],
            device_id={"tensor": peer},
            device_id_type=MESH,
        )
        copy.start()
        copies[k] = copy
    arrived[0] = send[me]

    for copy in loads[1:]:
        copy.wait()
    lang = language[me // 4]
    spread(lambda at, n: drafter[0, lang, :, at : at + n], shares, 0.0)
    total = jnp.sum(shares[...].reshape(CHUNKS * GROUP // 8, 8, LANES), axis=0)
    total = jnp.sum(total, axis=(0, 1), keepdims=True)
    inverse = 1.0 / total

    for r in range(4):
        attn_out[r] = attend(r, q, kv, fresh, used[r])

    place = lax.broadcasted_iota(jnp.int32, (CHUNKS, LANES), 0) * LANES + lax.broadcasted_iota(
        jnp.int32, (CHUNKS, LANES), 1
    )
    wanted = token[me]
    for k in (0,) + ORDER[::-1]:
        if k:
            copies[k].wait_recv()
        block = arrived[k].astype(jnp.float32).reshape(8, 8, LANES)
        peak = jnp.max(block, axis=0)
        peaks[k] = peak
        terms[k] = jnp.exp(block - peak[None])

    top = jnp.max(peaks[...], axis=0)
    top = jnp.max(top, axis=(0, 1), keepdims=True)
    norm = jnp.zeros((8, LANES), jnp.float32)
    for k in range(GROUP):
        norm = norm + jnp.sum(terms[k], axis=0) * jnp.exp(peaks[k] - top)
    norm = jnp.sum(norm, axis=(0, 1), keepdims=True)
    mass = jnp.zeros((8, LANES), jnp.float32)
    prob = jnp.zeros((8, LANES), jnp.float32)
    share = jnp.zeros((8, LANES), jnp.float32)
    for k in range(GROUP):
        piece = lax.rem(me + GROUP - k, GROUP)
        probs = terms[k] * (jnp.exp(peaks[k] - top) / norm)[None]
        drafted = shares[pl.ds(piece, CHUNKS, stride=GROUP), :].reshape(8, 8, LANES) * inverse[None]
        mass = mass + jnp.sum(jnp.maximum(probs - drafted, 0.0), axis=0)
        hit = (place == wanted - piece * VSHARD).reshape(8, 8, LANES)
        prob = prob + jnp.sum(jnp.where(hit, probs, 0.0), axis=0)
        share = share + jnp.sum(jnp.where(hit, drafted, 0.0), axis=0)
    mass = jnp.sum(mass, axis=(0, 1), keepdims=True)
    prob = jnp.sum(prob, axis=(0, 1), keepdims=True)
    share = jnp.sum(share, axis=(0, 1), keepdims=True)
    margin = jnp.minimum(1.0, prob / share) - uniform[me]

    lane = lax.broadcasted_iota(jnp.int32, (1, LANES), 1)
    row = jnp.where(lane == me, margin, 0.0) + jnp.where(lane == me + GROUP, mass, 0.0)
    stat[...] = row
    stat_copies = []
    for k in ORDER:
        peer = lax.rem(me + k, GROUP)
        copy = pltpu.make_async_remote_copy(
            src_ref=stat,
            dst_ref=stats.at[k - 1],
            send_sem=stat_send.at[k],
            recv_sem=stat_recv.at[k],
            device_id={"tensor": peer},
            device_id_type=MESH,
        )
        copy.start()
        stat_copies.append(copy)
    for k in ORDER:
        copies[k].wait_send()
    for copy in stat_copies:
        copy.wait()
    row = row + jnp.sum(stats[...], axis=0)
    margin_out[...] = row[0, 0:GROUP]
    mass_out[...] = row[0, GROUP : 2 * GROUP]


def on_device(
    queries, cache, new_kv, cache_len, target_logits, drafter, draft_tokens, language, uniforms
):
    anywhere = pl.BlockSpec(memory_space=pltpu.HBM)
    vmem = pl.BlockSpec(memory_space=pltpu.VMEM)
    f32 = jnp.float32
    bf16 = jnp.bfloat16
    return pl.pallas_call(
        kernel,
        out_shape=(
            jax.ShapeDtypeStruct(queries.shape, bf16),
            jax.ShapeDtypeStruct((GROUP,), f32),
            jax.ShapeDtypeStruct((GROUP,), f32),
        ),
        in_specs=[anywhere] * 9,
        out_specs=(vmem, vmem, vmem),
        scratch_shapes=[
            pltpu.VMEM(queries.shape, bf16),
            pltpu.VMEM(cache.shape, bf16),
            pltpu.VMEM(new_kv.shape, bf16),
            pltpu.VMEM(target_logits.shape, bf16),
            pltpu.VMEM(drafter.shape, bf16),
            pltpu.SMEM(cache_len.shape, jnp.int32),
            pltpu.SMEM(draft_tokens.shape, jnp.int32),
            pltpu.SMEM(language.shape, jnp.int32),
            pltpu.SMEM(uniforms.shape, f32),
            pltpu.VMEM((CHUNKS * GROUP, LANES), f32),
            pltpu.VMEM((CHUNKS * GROUP, LANES), f32),
            pltpu.VMEM((GROUP, CHUNKS, LANES), bf16),
            pltpu.VMEM((GROUP, CHUNKS, LANES), bf16),
            pltpu.VMEM((GROUP, 8, 8, LANES), f32),
            pltpu.VMEM((GROUP, 8, LANES), f32),
            pltpu.VMEM((1, LANES), f32),
            pltpu.VMEM((GROUP - 1, 1, LANES), f32),
            pltpu.SemaphoreType.DMA((9,)),
            pltpu.SemaphoreType.DMA((GROUP,)),
            pltpu.SemaphoreType.DMA((GROUP,)),
            pltpu.SemaphoreType.DMA((GROUP,)),
            pltpu.SemaphoreType.DMA((GROUP,)),
        ],
        compiler_params=pltpu.CompilerParams(
            collective_id=0, has_side_effects=True, vmem_limit_bytes=60 * 1024 * 1024
        ),
    )(queries, cache, new_kv, cache_len, target_logits, drafter, draft_tokens, language, uniforms)


def solution(mesh):
    in_specs = (
        P("dp", None, "tensor", None),
        P("tensor", "dp", None, None),
        P("tensor", "dp", None, None),
        P("dp"),
        P("dp", "tensor"),
        P(("dp", "tensor"), None, None, None),
        P("dp"),
        P("dp"),
        P("dp"),
    )
    out_specs = (P("dp", None, "tensor", None), P("dp"), P("dp"))
    return jax.shard_map(
        on_device, mesh=mesh, in_specs=in_specs, out_specs=out_specs, check_vma=False
    )
```

```python
import math

import jax
import jax.numpy as jnp
from jax import lax
from jax.experimental import pallas as pl
from jax.experimental.pallas import tpu as pltpu
from jax.sharding import PartitionSpec as P

MESH = pl.DeviceIdType.MESH
GROUP = 16
LANES = 128
VSHARD = 8016
FULL = VSHARD // LANES
TAIL = VSHARD - FULL * LANES
CHUNKS = 64
ABSENT = -3.0e38


def spread(load, tiles, fill):
    for c in range(FULL):
        tiles[pl.ds(GROUP * c, GROUP), :] = load(c * LANES, LANES).astype(jnp.float32)
    rest = (CHUNKS - FULL) * GROUP
    tiles[pl.ds(GROUP * FULL, rest), :] = jnp.full((rest, LANES), fill, jnp.float32)
    tiles[pl.ds(GROUP * FULL, GROUP), 0:TAIL] = load(FULL * LANES, TAIL).astype(jnp.float32)


def attend(r, q, kv, fresh, used):
    depth = q.shape[-1]
    scale = 1.0 / math.sqrt(depth)
    query = q[r].astype(jnp.float32).reshape(32, depth).astype(jnp.bfloat16)
    nt = (((1,), (1,)), ((), ()))
    nn = (((1,), (0,)), ((), ()))
    past = kv[0, r]
    new = fresh[0, r]
    past_scores = (
        lax.dot_general(query, past[:, :depth], nt, preferred_element_type=jnp.float32) * scale
    )
    new_scores = (
        lax.dot_general(query, new[:, :depth], nt, preferred_element_type=jnp.float32) * scale
    )
    position = lax.broadcasted_iota(jnp.int32, past_scores.shape, 1)
    past_scores = jnp.where(position < used, past_scores, -jnp.inf)
    draft = lax.broadcasted_iota(jnp.int32, new_scores.shape, 0) // 8
    key = lax.broadcasted_iota(jnp.int32, new_scores.shape, 1)
    new_scores = jnp.where(key <= draft, new_scores, -jnp.inf)
    peak = jnp.maximum(
        jnp.max(past_scores, axis=1, keepdims=True), jnp.max(new_scores, axis=1, keepdims=True)
    )
    past_exp = jnp.exp(past_scores - peak)
    new_exp = jnp.exp(new_scores - peak)
    total = jnp.sum(past_exp, axis=1, keepdims=True) + jnp.sum(new_exp, axis=1, keepdims=True)
    past_w = (past_exp / total).astype(jnp.bfloat16)
    new_w = (new_exp / total).astype(jnp.bfloat16)
    mixed = lax.dot_general(past_w, past[:, depth:], nn, preferred_element_type=jnp.float32)
    mixed = mixed + lax.dot_general(new_w, new[:, depth:], nn, preferred_element_type=jnp.float32)
    return mixed.reshape(4, 8, depth).astype(jnp.bfloat16)


def kernel(
    q_in,
    kv_in,
    fresh_in,
    used_in,
    logits_in,
    drafter_in,
    token_in,
    language_in,
    uniform_in,
    attn_out,
    row_out,
    q,
    kv,
    fresh,
    logits,
    drafter,
    used,
    token,
    language,
    uniform,
    tiles,
    shares,
    send,
    arrived,
    terms,
    peaks,
    norms,
    picks,
    stats,
    load_sem,
    send_sem,
    recv_sem,
    stat_send,
    stat_recv,
    ready,
):
    me = lax.axis_index("tensor")
    shift = jnp.where(lax.axis_index("dp") == 0, 1, 0)
    turn = lax.rem(me + (GROUP - 1) * shift, GROUP)

    def rank_at(turn):
        return lax.rem(turn + shift, GROUP)

    barrier = pltpu.get_barrier_semaphore()

    def greet(at, carry):
        peer = rank_at(at)
        pl.semaphore_signal(barrier, inc=1, device_id={"tensor": peer}, device_id_type=MESH)
        return carry

    lax.fori_loop(turn + 1, GROUP, greet, 0)

    loads = []
    for at, (src, dst) in enumerate(
        (
            (logits_in, logits),
            (language_in, language),
            (drafter_in, drafter),
            (token_in, token),
            (uniform_in, uniform),
            (used_in, used),
            (q_in, q),
            (kv_in, kv),
            (fresh_in, fresh),
        )
    ):
        copy = pltpu.make_async_copy(src, dst, load_sem.at[at])
        if at == 0:
            copy.start()
        loads.append(copy)

    @pl.when(turn > 0)
    def _():
        pl.semaphore_wait(barrier, turn)

    def announce(at, carry):
        peer = rank_at(at)
        pl.semaphore_signal(ready.at[me], inc=1, device_id={"tensor": peer}, device_id_type=MESH)
        return carry

    lax.fori_loop(0, turn, announce, 0)
    for copy in loads[1:]:
        copy.start()

    loads[0].wait()
    spread(lambda at, n: logits[:, at : at + n], tiles, ABSENT)
    for s in range(GROUP):
        send[s] = tiles[pl.ds(s, CHUNKS, stride=GROUP), :].astype(jnp.bfloat16)

    def block_to(peer):
        return pltpu.make_async_remote_copy(
            src_ref=send.at[peer],
            dst_ref=arrived.at[me],
            send_sem=send_sem.at[peer],
            recv_sem=recv_sem.at[me],
            device_id={"tensor": peer},
            device_id_type=MESH,
        )

    def block_from(peer):
        return pltpu.make_async_remote_copy(
            src_ref=send.at[peer],
            dst_ref=arrived.at[peer],
            send_sem=send_sem.at[peer],
            recv_sem=recv_sem.at[peer],
            device_id={"tensor": peer},
            device_id_type=MESH,
        )

    def send_down(at, carry):
        block_to(rank_at(at)).start()
        return carry

    lax.fori_loop(0, turn, send_down, 0)
    arrived[me] = send[me]

    for copy in loads[1:]:
        copy.wait()
    lang = language[me // 4]
    spread(lambda at, n: drafter[0, lang, :, at : at + n], tiles, 0.0)
    total = jnp.sum(tiles[...].reshape(CHUNKS * GROUP // 8, 8, LANES), axis=0)
    inverse = 1.0 / jnp.sum(total, axis=(0, 1), keepdims=True)
    place = lax.broadcasted_iota(jnp.int32, (CHUNKS, LANES), 0) * LANES + lax.broadcasted_iota(
        jnp.int32, (CHUNKS, LANES), 1
    )
    wanted = token[me]
    share = jnp.zeros((8, LANES), jnp.float32)
    for p in range(GROUP):
        drafted = tiles[pl.ds(p, CHUNKS, stride=GROUP), :] * inverse
        hit = place == wanted - p * VSHARD
        share = share + jnp.sum(jnp.where(hit, drafted, 0.0).reshape(8, 8, LANES), axis=0)
        shares[p] = drafted.reshape(8, 8, LANES)
    share = jnp.sum(share, axis=(0, 1), keepdims=True)

    for r in range(4):
        attn_out[r] = attend(r, q, kv, fresh, used[r])

    def send_up(at, carry):
        peer = rank_at(at)
        pl.semaphore_wait(ready.at[peer], 1)
        block_to(peer).start()
        return carry

    lax.fori_loop(turn + 1, GROUP, send_up, 0)

    def digest(peer):
        block = arrived[peer].astype(jnp.float32).reshape(8, 8, LANES)
        peak = jnp.max(block, axis=0)
        term = jnp.exp(block - peak[None])
        hit = (place == wanted - peer * VSHARD).reshape(8, 8, LANES)
        peaks[peer] = peak
        terms[peer] = term
        norms[peer] = jnp.sum(term, axis=0)
        picks[peer] = jnp.sum(jnp.where(hit, term, 0.0), axis=0)

    def receive(at, carry):
        peer = rank_at(at)
        block_from(peer).wait_recv()
        digest(peer)
        return carry

    digest(me)
    lax.fori_loop(0, turn, receive, 0)
    lax.fori_loop(turn + 1, GROUP, receive, 0)

    top = jnp.max(peaks[...], axis=0)
    top = jnp.max(top, axis=(0, 1), keepdims=True)
    scales = jnp.exp(peaks[...] - top[None])
    norm = jnp.sum(norms[...] * scales, axis=0)
    scales = scales * (1.0 / jnp.sum(norm, axis=(0, 1), keepdims=True))[None]
    prob = jnp.sum(picks[...] * scales, axis=0)
    mass = jnp.zeros((8, LANES), jnp.float32)
    for p in range(GROUP):
        mass = mass + jnp.sum(jnp.maximum(terms[p] * scales[p][None] - shares[p], 0.0), axis=0)
    mass = jnp.sum(mass, axis=(0, 1), keepdims=True)
    prob = jnp.sum(prob, axis=(0, 1), keepdims=True)
    margin = jnp.minimum(1.0, prob / share) - uniform[me]

    lane = lax.broadcasted_iota(jnp.int32, (1, LANES), 1)
    row = jnp.where(lane == me, margin, 0.0) + jnp.where(lane == me + GROUP, mass, 0.0)
    stats[me] = row

    def stat_to(peer):
        return pltpu.make_async_remote_copy(
            src_ref=stats.at[me],
            dst_ref=stats.at[me],
            send_sem=stat_send.at[peer],
            recv_sem=stat_recv.at[me],
            device_id={"tensor": peer},
            device_id_type=MESH,
        )

    def stat_start(peer, carry):
        stat_to(peer).start()
        return carry

    lax.fori_loop(0, me, stat_start, 0)
    lax.fori_loop(me + 1, GROUP, stat_start, 0)

    def sent(peer, carry):
        block_to(peer).wait_send()
        return carry

    lax.fori_loop(0, me, sent, 0)
    lax.fori_loop(me + 1, GROUP, sent, 0)

    def stat_done(peer, carry):
        pltpu.make_async_remote_copy(
            src_ref=stats.at[me],
            dst_ref=stats.at[peer],
            send_sem=stat_send.at[peer],
            recv_sem=stat_recv.at[peer],
            device_id={"tensor": peer},
            device_id_type=MESH,
        ).wait()
        return carry

    lax.fori_loop(0, me, stat_done, 0)
    lax.fori_loop(me + 1, GROUP, stat_done, 0)
    row_out[...] = jnp.sum(stats[...], axis=0)


def on_device(
    queries, cache, new_kv, cache_len, target_logits, drafter, draft_tokens, language, uniforms
):
    anywhere = pl.BlockSpec(memory_space=pltpu.HBM)
    vmem = pl.BlockSpec(memory_space=pltpu.VMEM)
    f32 = jnp.float32
    bf16 = jnp.bfloat16
    attn, row = pl.pallas_call(
        kernel,
        out_shape=(
            pltpu.VMEM(queries.shape, bf16),
            pltpu.VMEM((1, LANES), f32),
        ),
        in_specs=[anywhere] * 9,
        out_specs=(vmem, vmem),
        scratch_shapes=[
            pltpu.VMEM(queries.shape, bf16),
            pltpu.VMEM(cache.shape, bf16),
            pltpu.VMEM(new_kv.shape, bf16),
            pltpu.VMEM(target_logits.shape, bf16),
            pltpu.VMEM(drafter.shape, bf16),
            pltpu.SMEM(cache_len.shape, jnp.int32),
            pltpu.SMEM(draft_tokens.shape, jnp.int32),
            pltpu.SMEM(language.shape, jnp.int32),
            pltpu.SMEM(uniforms.shape, f32),
            pltpu.VMEM((CHUNKS * GROUP, LANES), f32),
            pltpu.VMEM((GROUP, 8, 8, LANES), f32),
            pltpu.VMEM((GROUP, CHUNKS, LANES), bf16),
            pltpu.VMEM((GROUP, CHUNKS, LANES), bf16),
            pltpu.VMEM((GROUP, 8, 8, LANES), f32),
            pltpu.VMEM((GROUP, 8, LANES), f32),
            pltpu.VMEM((GROUP, 8, LANES), f32),
            pltpu.VMEM((GROUP, 8, LANES), f32),
            pltpu.VMEM((GROUP, 1, LANES), f32),
            pltpu.SemaphoreType.DMA((9,)),
            pltpu.SemaphoreType.DMA((GROUP,)),
            pltpu.SemaphoreType.DMA((GROUP,)),
            pltpu.SemaphoreType.DMA((GROUP,)),
            pltpu.SemaphoreType.DMA((GROUP,)),
            pltpu.SemaphoreType.REGULAR((GROUP,)),
        ],
        compiler_params=pltpu.CompilerParams(
            collective_id=0, has_side_effects=True, vmem_limit_bytes=60 * 1024 * 1024
        ),
    )(queries, cache, new_kv, cache_len, target_logits, drafter, draft_tokens, language, uniforms)
    return attn, row[0, :GROUP], row[0, GROUP : 2 * GROUP]


def solution(mesh):
    in_specs = (
        P("dp", None, "tensor", None),
        P("tensor", "dp", None, None),
        P("tensor", "dp", None, None),
        P("dp"),
        P("dp", "tensor"),
        P(("dp", "tensor"), None, None, None),
        P("dp"),
        P("dp"),
        P("dp"),
    )
    out_specs = (P("dp", None, "tensor", None), P("dp"), P("dp"))
    return jax.shard_map(
        on_device, mesh=mesh, in_specs=in_specs, out_specs=out_specs, check_vma=False
    )
```

```python
import math

import jax
import jax.numpy as jnp
from jax import lax
from jax.experimental import pallas as pl
from jax.experimental.pallas import tpu as pltpu
from jax.sharding import PartitionSpec as P

MESH = pl.DeviceIdType.MESH
GROUP = 16
LANES = 128
VSHARD = 8016
FULL = VSHARD // LANES
TAIL = VSHARD - FULL * LANES
CHUNKS = 64
ABSENT = -3.0e38


def spread(load, tiles, fill):
    for c in range(FULL):
        tiles[pl.ds(GROUP * c, GROUP), :] = load(c * LANES, LANES).astype(jnp.float32)
    rest = (CHUNKS - FULL) * GROUP
    tiles[pl.ds(GROUP * FULL, rest), :] = jnp.full((rest, LANES), fill, jnp.float32)
    tiles[pl.ds(GROUP * FULL, GROUP), 0:TAIL] = load(FULL * LANES, TAIL).astype(jnp.float32)


def attend(r, q, kv, fresh, used):
    depth = q.shape[-1]
    scale = 1.0 / math.sqrt(depth)
    query = q[r].astype(jnp.float32).reshape(32, depth).astype(jnp.bfloat16)
    nt = (((1,), (1,)), ((), ()))
    nn = (((1,), (0,)), ((), ()))
    past = kv[0, r]
    new = fresh[0, r]
    past_scores = (
        lax.dot_general(query, past[:, :depth], nt, preferred_element_type=jnp.float32) * scale
    )
    new_scores = (
        lax.dot_general(query, new[:, :depth], nt, preferred_element_type=jnp.float32) * scale
    )
    position = lax.broadcasted_iota(jnp.int32, past_scores.shape, 1)
    past_scores = jnp.where(position < used, past_scores, -jnp.inf)
    draft = lax.broadcasted_iota(jnp.int32, new_scores.shape, 0) // 8
    key = lax.broadcasted_iota(jnp.int32, new_scores.shape, 1)
    new_scores = jnp.where(key <= draft, new_scores, -jnp.inf)
    peak = jnp.maximum(
        jnp.max(past_scores, axis=1, keepdims=True), jnp.max(new_scores, axis=1, keepdims=True)
    )
    past_exp = jnp.exp(past_scores - peak)
    new_exp = jnp.exp(new_scores - peak)
    total = jnp.sum(past_exp, axis=1, keepdims=True) + jnp.sum(new_exp, axis=1, keepdims=True)
    past_w = (past_exp / total).astype(jnp.bfloat16)
    new_w = (new_exp / total).astype(jnp.bfloat16)
    mixed = lax.dot_general(past_w, past[:, depth:], nn, preferred_element_type=jnp.float32)
    mixed = mixed + lax.dot_general(new_w, new[:, depth:], nn, preferred_element_type=jnp.float32)
    return mixed.reshape(4, 8, depth).astype(jnp.bfloat16)


def kernel(
    q_in,
    kv_in,
    fresh_in,
    used_in,
    logits_in,
    drafter_in,
    token_in,
    language_in,
    uniform_in,
    attn_out,
    row_out,
    q,
    kv,
    fresh,
    logits,
    drafter,
    used,
    token,
    language,
    uniform,
    tiles,
    shares,
    send,
    arrived,
    terms,
    peaks,
    norms,
    picks,
    stats,
    load_sem,
    send_sem,
    recv_sem,
    stat_send,
    stat_recv,
    ready,
):
    me = lax.axis_index("tensor")
    shift = jnp.where(lax.axis_index("dp") == 0, 1, 0)
    turn = lax.rem(me + (GROUP - 1) * shift, GROUP)

    def rank_at(turn):
        return lax.rem(turn + shift, GROUP)

    def far_first(at):
        near = (at + 1) // 2
        return lax.rem(me + 8 + near * (1 - 2 * ((at + 1) % 2)), GROUP)

    def turn_of(rank):
        return lax.rem(rank + (GROUP - 1) * shift, GROUP)

    barrier = pltpu.get_barrier_semaphore()

    def greet(at, carry):
        peer = rank_at(at)
        pl.semaphore_signal(barrier, inc=1, device_id={"tensor": peer}, device_id_type=MESH)
        return carry

    lax.fori_loop(turn + 1, GROUP, greet, 0)

    loads = []
    for at, (src, dst) in enumerate(
        (
            (logits_in, logits),
            (language_in, language),
            (drafter_in, drafter),
            (token_in, token),
            (uniform_in, uniform),
            (used_in, used),
            (q_in, q),
            (kv_in, kv),
            (fresh_in, fresh),
        )
    ):
        copy = pltpu.make_async_copy(src, dst, load_sem.at[at])
        if at == 0:
            copy.start()
        loads.append(copy)

    @pl.when(turn > 0)
    def _():
        pl.semaphore_wait(barrier, turn)

    def announce(at, carry):
        peer = far_first(at)

        @pl.when(turn_of(peer) < turn)
        def _():
            pl.semaphore_signal(
                ready.at[me], inc=1, device_id={"tensor": peer}, device_id_type=MESH
            )

        return carry

    lax.fori_loop(0, GROUP - 1, announce, 0)
    for copy in loads[1:]:
        copy.start()

    loads[0].wait()
    spread(lambda at, n: logits[:, at : at + n], tiles, ABSENT)

    def pack(slot):
        send[slot] = tiles[pl.ds(slot, CHUNKS, stride=GROUP), :].astype(jnp.bfloat16)


    def block_to(peer):
        return pltpu.make_async_remote_copy(
            src_ref=send.at[peer],
            dst_ref=arrived.at[me],
            send_sem=send_sem.at[peer],
            recv_sem=recv_sem.at[me],
            device_id={"tensor": peer},
            device_id_type=MESH,
        )

    def block_from(peer):
        return pltpu.make_async_remote_copy(
            src_ref=send.at[peer],
            dst_ref=arrived.at[peer],
            send_sem=send_sem.at[peer],
            recv_sem=recv_sem.at[peer],
            device_id={"tensor": peer},
            device_id_type=MESH,
        )

    def send_down(at, carry):
        peer = far_first(at)
        pack(peer)

        @pl.when(turn_of(peer) < turn)
        def _():
            block_to(peer).start()

        return carry

    lax.fori_loop(0, GROUP - 1, send_down, 0)
    arrived[me] = tiles[pl.ds(me, CHUNKS, stride=GROUP), :].astype(jnp.bfloat16)

    for copy in loads[1:]:
        copy.wait()
    lang = language[me // 4]
    spread(lambda at, n: drafter[0, lang, :, at : at + n], tiles, 0.0)
    total = jnp.sum(tiles[...].reshape(CHUNKS * GROUP // 8, 8, LANES), axis=0)
    inverse = 1.0 / jnp.sum(total, axis=(0, 1), keepdims=True)
    place = lax.broadcasted_iota(jnp.int32, (CHUNKS, LANES), 0) * LANES + lax.broadcasted_iota(
        jnp.int32, (CHUNKS, LANES), 1
    )
    wanted = token[me]
    share = jnp.zeros((8, LANES), jnp.float32)
    for p in range(GROUP):
        drafted = tiles[pl.ds(p, CHUNKS, stride=GROUP), :] * inverse
        hit = place == wanted - p * VSHARD
        share = share + jnp.sum(jnp.where(hit, drafted, 0.0).reshape(8, 8, LANES), axis=0)
        shares[p] = drafted.reshape(8, 8, LANES)
    share = jnp.sum(share, axis=(0, 1), keepdims=True)

    for r in range(4):
        attn_out[r] = attend(r, q, kv, fresh, used[r])

    def send_up(at, carry):
        peer = rank_at(at)
        pl.semaphore_wait(ready.at[peer], 1)
        block_to(peer).start()
        return carry

    lax.fori_loop(turn + 1, GROUP, send_up, 0)

    def digest(peer):
        block = arrived[peer].astype(jnp.float32).reshape(8, 8, LANES)
        peak = jnp.max(block, axis=0)
        term = jnp.exp(block - peak[None])
        hit = (place == wanted - peer * VSHARD).reshape(8, 8, LANES)
        peaks[peer] = peak
        terms[peer] = term
        norms[peer] = jnp.sum(term, axis=0)
        picks[peer] = jnp.sum(jnp.where(hit, term, 0.0), axis=0)

    def receive(at, carry):
        peer = rank_at(at)
        block_from(peer).wait_recv()
        digest(peer)
        return carry

    digest(me)
    lax.fori_loop(0, turn, receive, 0)
    lax.fori_loop(turn + 1, GROUP, receive, 0)

    top = jnp.max(peaks[...], axis=0)
    top = jnp.max(top, axis=(0, 1), keepdims=True)
    scales = jnp.exp(peaks[...] - top[None])
    norm = jnp.sum(norms[...] * scales, axis=0)
    scales = scales * (1.0 / jnp.sum(norm, axis=(0, 1), keepdims=True))[None]
    prob = jnp.sum(picks[...] * scales, axis=0)
    mass = jnp.zeros((8, LANES), jnp.float32)
    for p in range(GROUP):
        mass = mass + jnp.sum(jnp.maximum(terms[p] * scales[p][None] - shares[p], 0.0), axis=0)
    mass = jnp.sum(mass, axis=(0, 1), keepdims=True)
    prob = jnp.sum(prob, axis=(0, 1), keepdims=True)
    margin = jnp.minimum(1.0, prob / share) - uniform[me]

    lane = lax.broadcasted_iota(jnp.int32, (1, LANES), 1)
    row = jnp.where(lane == me, margin, 0.0) + jnp.where(lane == me + GROUP, mass, 0.0)
    stats[me] = row

    def stat_to(peer):
        return pltpu.make_async_remote_copy(
            src_ref=stats.at[me],
            dst_ref=stats.at[me],
            send_sem=stat_send.at[peer],
            recv_sem=stat_recv.at[me],
            device_id={"tensor": peer},
            device_id_type=MESH,
        )

    def stat_start(peer, carry):
        stat_to(peer).start()
        return carry

    lax.fori_loop(0, me, stat_start, 0)
    lax.fori_loop(me + 1, GROUP, stat_start, 0)

    def sent(peer, carry):
        block_to(peer).wait_send()
        return carry

    lax.fori_loop(0, me, sent, 0)
    lax.fori_loop(me + 1, GROUP, sent, 0)

    def stat_done(peer, carry):
        pltpu.make_async_remote_copy(
            src_ref=stats.at[me],
            dst_ref=stats.at[peer],
            send_sem=stat_send.at[peer],
            recv_sem=stat_recv.at[peer],
            device_id={"tensor": peer},
            device_id_type=MESH,
        ).wait()
        return carry

    lax.fori_loop(0, me, stat_done, 0)
    lax.fori_loop(me + 1, GROUP, stat_done, 0)
    row_out[...] = jnp.sum(stats[...], axis=0)


def on_device(
    queries, cache, new_kv, cache_len, target_logits, drafter, draft_tokens, language, uniforms
):
    anywhere = pl.BlockSpec(memory_space=pltpu.HBM)
    vmem = pl.BlockSpec(memory_space=pltpu.VMEM)
    f32 = jnp.float32
    bf16 = jnp.bfloat16
    attn, row = pl.pallas_call(
        kernel,
        out_shape=(
            pltpu.VMEM(queries.shape, bf16),
            pltpu.VMEM((1, LANES), f32),
        ),
        in_specs=[anywhere] * 9,
        out_specs=(vmem, vmem),
        scratch_shapes=[
            pltpu.VMEM(queries.shape, bf16),
            pltpu.VMEM(cache.shape, bf16),
            pltpu.VMEM(new_kv.shape, bf16),
            pltpu.VMEM(target_logits.shape, bf16),
            pltpu.VMEM(drafter.shape, bf16),
            pltpu.SMEM(cache_len.shape, jnp.int32),
            pltpu.SMEM(draft_tokens.shape, jnp.int32),
            pltpu.SMEM(language.shape, jnp.int32),
            pltpu.SMEM(uniforms.shape, f32),
            pltpu.VMEM((CHUNKS * GROUP, LANES), f32),
            pltpu.VMEM((GROUP, 8, 8, LANES), f32),
            pltpu.VMEM((GROUP, CHUNKS, LANES), bf16),
            pltpu.VMEM((GROUP, CHUNKS, LANES), bf16),
            pltpu.VMEM((GROUP, 8, 8, LANES), f32),
            pltpu.VMEM((GROUP, 8, LANES), f32),
            pltpu.VMEM((GROUP, 8, LANES), f32),
            pltpu.VMEM((GROUP, 8, LANES), f32),
            pltpu.VMEM((GROUP, 1, LANES), f32),
            pltpu.SemaphoreType.DMA((9,)),
            pltpu.SemaphoreType.DMA((GROUP,)),
            pltpu.SemaphoreType.DMA((GROUP,)),
            pltpu.SemaphoreType.DMA((GROUP,)),
            pltpu.SemaphoreType.DMA((GROUP,)),
            pltpu.SemaphoreType.REGULAR((GROUP,)),
        ],
        compiler_params=pltpu.CompilerParams(
            collective_id=0, has_side_effects=True, vmem_limit_bytes=60 * 1024 * 1024
        ),
    )(queries, cache, new_kv, cache_len, target_logits, drafter, draft_tokens, language, uniforms)
    return attn, row[0, :GROUP], row[0, GROUP : 2 * GROUP]


def solution(mesh):
    in_specs = (
        P("dp", None, "tensor", None),
        P("tensor", "dp", None, None),
        P("tensor", "dp", None, None),
        P("dp"),
        P("dp", "tensor"),
        P(("dp", "tensor"), None, None, None),
        P("dp"),
        P("dp"),
        P("dp"),
    )
    out_specs = (P("dp", None, "tensor", None), P("dp"), P("dp"))
    return jax.shard_map(
        on_device, mesh=mesh, in_specs=in_specs, out_specs=out_specs, check_vma=False
    )
```

```python
import math

import jax
import jax.numpy as jnp
from jax import lax
from jax.experimental import pallas as pl
from jax.experimental.pallas import tpu as pltpu
from jax.sharding import PartitionSpec as P

MESH = pl.DeviceIdType.MESH
GROUP = 16
LANES = 128
VSHARD = 8016
FULL = VSHARD // LANES
TAIL = VSHARD - FULL * LANES
CHUNKS = 64
ABSENT = -3.0e38


def spread(load, tiles, fill):
    for c in range(FULL):
        tiles[pl.ds(GROUP * c, GROUP), :] = load(c * LANES, LANES).astype(jnp.float32)
    rest = (CHUNKS - FULL) * GROUP
    tiles[pl.ds(GROUP * FULL, rest), :] = jnp.full((rest, LANES), fill, jnp.float32)
    tiles[pl.ds(GROUP * FULL, GROUP), 0:TAIL] = load(FULL * LANES, TAIL).astype(jnp.float32)


def attend(r, q, kv, fresh, used):
    depth = q.shape[-1]
    scale = 1.0 / math.sqrt(depth)
    query = q[r].astype(jnp.float32).reshape(32, depth).astype(jnp.bfloat16)
    nt = (((1,), (1,)), ((), ()))
    nn = (((1,), (0,)), ((), ()))
    past = kv[0, r]
    new = fresh[0, r]
    past_scores = (
        lax.dot_general(query, past[:, :depth], nt, preferred_element_type=jnp.float32) * scale
    )
    new_scores = (
        lax.dot_general(query, new[:, :depth], nt, preferred_element_type=jnp.float32) * scale
    )
    position = lax.broadcasted_iota(jnp.int32, past_scores.shape, 1)
    past_scores = jnp.where(position < used, past_scores, -jnp.inf)
    draft = lax.broadcasted_iota(jnp.int32, new_scores.shape, 0) // 8
    key = lax.broadcasted_iota(jnp.int32, new_scores.shape, 1)
    new_scores = jnp.where(key <= draft, new_scores, -jnp.inf)
    peak = jnp.maximum(
        jnp.max(past_scores, axis=1, keepdims=True), jnp.max(new_scores, axis=1, keepdims=True)
    )
    past_exp = jnp.exp(past_scores - peak)
    new_exp = jnp.exp(new_scores - peak)
    total = jnp.sum(past_exp, axis=1, keepdims=True) + jnp.sum(new_exp, axis=1, keepdims=True)
    past_w = (past_exp / total).astype(jnp.bfloat16)
    new_w = (new_exp / total).astype(jnp.bfloat16)
    mixed = lax.dot_general(past_w, past[:, depth:], nn, preferred_element_type=jnp.float32)
    mixed = mixed + lax.dot_general(new_w, new[:, depth:], nn, preferred_element_type=jnp.float32)
    return mixed.reshape(4, 8, depth).astype(jnp.bfloat16)


def kernel(
    q_in,
    kv_in,
    fresh_in,
    used_in,
    logits_in,
    drafter_in,
    token_in,
    language_in,
    uniform_in,
    attn_out,
    row_out,
    q,
    kv,
    fresh,
    logits,
    drafter,
    used,
    token,
    language,
    uniform,
    tiles,
    shares,
    send,
    arrived,
    terms,
    peaks,
    norms,
    picks,
    stats,
    load_sem,
    send_sem,
    recv_sem,
    stat_send,
    stat_recv,
    ready,
):
    me = lax.axis_index("tensor")
    shift = jnp.where(lax.axis_index("dp") == 0, 1, 0)
    turn = lax.rem(me + (GROUP - 1) * shift, GROUP)

    def rank_at(turn):
        return lax.rem(turn + shift, GROUP)

    def far_first(at):
        near = (at + 1) // 2
        return lax.rem(me + 8 + near * (1 - 2 * ((at + 1) % 2)), GROUP)

    def turn_of(rank):
        return lax.rem(rank + (GROUP - 1) * shift, GROUP)

    barrier = pltpu.get_barrier_semaphore()

    def greet(at, carry):
        peer = rank_at(at)
        pl.semaphore_signal(barrier, inc=1, device_id={"tensor": peer}, device_id_type=MESH)
        return carry

    lax.fori_loop(turn + 1, GROUP, greet, 0)

    loads = []
    for at, (src, dst) in enumerate(
        (
            (logits_in.at[:, :2048], logits.at[:, :2048]),
            (logits_in.at[:, 2048:4096], logits.at[:, 2048:4096]),
            (logits_in.at[:, 4096:6144], logits.at[:, 4096:6144]),
            (logits_in.at[:, 6144:], logits.at[:, 6144:]),
            (language_in, language),
            (drafter_in, drafter),
            (token_in, token),
            (uniform_in, uniform),
            (used_in, used),
            (q_in, q),
            (kv_in, kv),
            (fresh_in, fresh),
        )
    ):
        copy = pltpu.make_async_copy(src, dst, load_sem.at[at])
        if at < 4:
            copy.start()
        loads.append(copy)

    @pl.when(turn > 0)
    def _():
        pl.semaphore_wait(barrier, turn)

    def announce(at, carry):
        peer = far_first(at)

        @pl.when(turn_of(peer) < turn)
        def _():
            pl.semaphore_signal(
                ready.at[me], inc=1, device_id={"tensor": peer}, device_id_type=MESH
            )

        return carry

    lax.fori_loop(0, GROUP - 1, announce, 0)
    for copy in loads[4:]:
        copy.start()

    def logit_tile(at, n):
        if at % 2048 == 0:
            loads[at // 2048].wait()
        return logits[:, at : at + n]

    spread(logit_tile, tiles, ABSENT)

    def pack(slot):
        send[slot] = tiles[pl.ds(slot, CHUNKS, stride=GROUP), :].astype(jnp.bfloat16)


    def block_to(peer):
        return pltpu.make_async_remote_copy(
            src_ref=send.at[peer],
            dst_ref=arrived.at[me],
            send_sem=send_sem.at[peer],
            recv_sem=recv_sem.at[me],
            device_id={"tensor": peer},
            device_id_type=MESH,
        )

    def block_from(peer):
        return pltpu.make_async_remote_copy(
            src_ref=send.at[peer],
            dst_ref=arrived.at[peer],
            send_sem=send_sem.at[peer],
            recv_sem=recv_sem.at[peer],
            device_id={"tensor": peer},
            device_id_type=MESH,
        )

    def send_down(at, carry):
        peer = far_first(at)
        pack(peer)

        @pl.when(turn_of(peer) < turn)
        def _():
            block_to(peer).start()

        return carry

    lax.fori_loop(0, GROUP - 1, send_down, 0)
    arrived[me] = tiles[pl.ds(me, CHUNKS, stride=GROUP), :].astype(jnp.bfloat16)

    def send_up(at, carry):
        peer = rank_at(at)
        pl.semaphore_wait(ready.at[peer], 1)
        block_to(peer).start()
        return carry

    lax.fori_loop(turn + 1, GROUP, send_up, 0)

    for copy in loads[4:]:
        copy.wait()
    lang = language[me // 4]
    spread(lambda at, n: drafter[0, lang, :, at : at + n], tiles, 0.0)
    total = jnp.sum(tiles[...].reshape(CHUNKS * GROUP // 8, 8, LANES), axis=0)
    inverse = 1.0 / jnp.sum(total, axis=(0, 1), keepdims=True)
    place = lax.broadcasted_iota(jnp.int32, (CHUNKS, LANES), 0) * LANES + lax.broadcasted_iota(
        jnp.int32, (CHUNKS, LANES), 1
    )
    wanted = token[me]
    share = jnp.zeros((8, LANES), jnp.float32)
    for p in range(GROUP):
        drafted = tiles[pl.ds(p, CHUNKS, stride=GROUP), :] * inverse
        hit = place == wanted - p * VSHARD
        share = share + jnp.sum(jnp.where(hit, drafted, 0.0).reshape(8, 8, LANES), axis=0)
        shares[p] = drafted.reshape(8, 8, LANES)
    share = jnp.sum(share, axis=(0, 1), keepdims=True)

    for r in range(4):
        attn_out[r] = attend(r, q, kv, fresh, used[r])

    def digest(peer):
        block = arrived[peer].astype(jnp.float32).reshape(8, 8, LANES)
        peak = jnp.max(block, axis=0)
        term = jnp.exp(block - peak[None])
        hit = (place == wanted - peer * VSHARD).reshape(8, 8, LANES)
        peaks[peer] = peak
        terms[peer] = term
        norms[peer] = jnp.sum(term, axis=0)
        picks[peer] = jnp.sum(jnp.where(hit, term, 0.0), axis=0)

    def receive(at, carry):
        peer = rank_at(at)
        block_from(peer).wait_recv()
        digest(peer)
        return carry

    digest(me)
    lax.fori_loop(0, turn, receive, 0)
    lax.fori_loop(turn + 1, GROUP, receive, 0)

    top = jnp.max(peaks[...], axis=0)
    top = jnp.max(top, axis=(0, 1), keepdims=True)
    scales = jnp.exp(peaks[...] - top[None])
    norm = jnp.sum(norms[...] * scales, axis=0)
    scales = scales * (1.0 / jnp.sum(norm, axis=(0, 1), keepdims=True))[None]
    prob = jnp.sum(picks[...] * scales, axis=0)
    mass = jnp.zeros((8, LANES), jnp.float32)
    for p in range(GROUP):
        mass = mass + jnp.sum(jnp.maximum(terms[p] * scales[p][None] - shares[p], 0.0), axis=0)
    mass = jnp.sum(mass, axis=(0, 1), keepdims=True)
    prob = jnp.sum(prob, axis=(0, 1), keepdims=True)
    margin = jnp.minimum(1.0, prob / share) - uniform[me]

    lane = lax.broadcasted_iota(jnp.int32, (1, LANES), 1)
    row = jnp.where(lane == me, margin, 0.0) + jnp.where(lane == me + GROUP, mass, 0.0)
    stats[me] = row

    def stat_to(peer):
        return pltpu.make_async_remote_copy(
            src_ref=stats.at[me],
            dst_ref=stats.at[me],
            send_sem=stat_send.at[peer],
            recv_sem=stat_recv.at[me],
            device_id={"tensor": peer},
            device_id_type=MESH,
        )

    def stat_start(peer, carry):
        stat_to(peer).start()
        return carry

    lax.fori_loop(0, me, stat_start, 0)
    lax.fori_loop(me + 1, GROUP, stat_start, 0)

    def sent(peer, carry):
        block_to(peer).wait_send()
        return carry

    lax.fori_loop(0, me, sent, 0)
    lax.fori_loop(me + 1, GROUP, sent, 0)

    def stat_done(peer, carry):
        pltpu.make_async_remote_copy(
            src_ref=stats.at[me],
            dst_ref=stats.at[peer],
            send_sem=stat_send.at[peer],
            recv_sem=stat_recv.at[peer],
            device_id={"tensor": peer},
            device_id_type=MESH,
        ).wait()
        return carry

    lax.fori_loop(0, me, stat_done, 0)
    lax.fori_loop(me + 1, GROUP, stat_done, 0)
    row_out[...] = jnp.sum(stats[...], axis=0)


def on_device(
    queries, cache, new_kv, cache_len, target_logits, drafter, draft_tokens, language, uniforms
):
    anywhere = pl.BlockSpec(memory_space=pltpu.HBM)
    vmem = pl.BlockSpec(memory_space=pltpu.VMEM)
    f32 = jnp.float32
    bf16 = jnp.bfloat16
    attn, row = pl.pallas_call(
        kernel,
        out_shape=(
            pltpu.VMEM(queries.shape, bf16),
            pltpu.VMEM((1, LANES), f32),
        ),
        in_specs=[anywhere] * 9,
        out_specs=(vmem, vmem),
        scratch_shapes=[
            pltpu.VMEM(queries.shape, bf16),
            pltpu.VMEM(cache.shape, bf16),
            pltpu.VMEM(new_kv.shape, bf16),
            pltpu.VMEM(target_logits.shape, bf16),
            pltpu.VMEM(drafter.shape, bf16),
            pltpu.SMEM(cache_len.shape, jnp.int32),
            pltpu.SMEM(draft_tokens.shape, jnp.int32),
            pltpu.SMEM(language.shape, jnp.int32),
            pltpu.SMEM(uniforms.shape, f32),
            pltpu.VMEM((CHUNKS * GROUP, LANES), f32),
            pltpu.VMEM((GROUP, 8, 8, LANES), f32),
            pltpu.VMEM((GROUP, CHUNKS, LANES), bf16),
            pltpu.VMEM((GROUP, CHUNKS, LANES), bf16),
            pltpu.VMEM((GROUP, 8, 8, LANES), f32),
            pltpu.VMEM((GROUP, 8, LANES), f32),
            pltpu.VMEM((GROUP, 8, LANES), f32),
            pltpu.VMEM((GROUP, 8, LANES), f32),
            pltpu.VMEM((GROUP, 1, LANES), f32),
            pltpu.SemaphoreType.DMA((12,)),
            pltpu.SemaphoreType.DMA((GROUP,)),
            pltpu.SemaphoreType.DMA((GROUP,)),
            pltpu.SemaphoreType.DMA((GROUP,)),
            pltpu.SemaphoreType.DMA((GROUP,)),
            pltpu.SemaphoreType.REGULAR((GROUP,)),
        ],
        compiler_params=pltpu.CompilerParams(
            collective_id=0, has_side_effects=True, vmem_limit_bytes=60 * 1024 * 1024
        ),
    )(queries, cache, new_kv, cache_len, target_logits, drafter, draft_tokens, language, uniforms)
    return attn, row[0, :GROUP], row[0, GROUP : 2 * GROUP]


def solution(mesh):
    in_specs = (
        P("dp", None, "tensor", None),
        P("tensor", "dp", None, None),
        P("tensor", "dp", None, None),
        P("dp"),
        P("dp", "tensor"),
        P(("dp", "tensor"), None, None, None),
        P("dp"),
        P("dp"),
        P("dp"),
    )
    out_specs = (P("dp", None, "tensor", None), P("dp"), P("dp"))
    return jax.shard_map(
        on_device, mesh=mesh, in_specs=in_specs, out_specs=out_specs, check_vma=False
    )
```

```python
import math

import jax
import jax.numpy as jnp
from jax import lax
from jax.experimental import pallas as pl
from jax.experimental.pallas import tpu as pltpu
from jax.sharding import PartitionSpec as P

MESH = pl.DeviceIdType.MESH
GROUP = 16
LANES = 128
VSHARD = 8016
FULL = VSHARD // LANES
TAIL = VSHARD - FULL * LANES
CHUNKS = 64
ABSENT = -3.0e38


def spread(load, tiles, fill):
    for c in range(FULL):
        tiles[pl.ds(GROUP * c, GROUP), :] = load(c * LANES, LANES).astype(jnp.float32)
    rest = (CHUNKS - FULL) * GROUP
    tiles[pl.ds(GROUP * FULL, rest), :] = jnp.full((rest, LANES), fill, jnp.float32)
    tiles[pl.ds(GROUP * FULL, GROUP), 0:TAIL] = load(FULL * LANES, TAIL).astype(jnp.float32)


def attend(r, q, kv, fresh, used):
    depth = q.shape[-1]
    scale = 1.0 / math.sqrt(depth)
    query = q[r].astype(jnp.float32).reshape(32, depth).astype(jnp.bfloat16)
    nt = (((1,), (1,)), ((), ()))
    nn = (((1,), (0,)), ((), ()))
    past = kv[0, r]
    new = fresh[0, r]
    past_scores = (
        lax.dot_general(query, past[:, :depth], nt, preferred_element_type=jnp.float32) * scale
    )
    new_scores = (
        lax.dot_general(query, new[:, :depth], nt, preferred_element_type=jnp.float32) * scale
    )
    position = lax.broadcasted_iota(jnp.int32, past_scores.shape, 1)
    past_scores = jnp.where(position < used, past_scores, -jnp.inf)
    draft = lax.broadcasted_iota(jnp.int32, new_scores.shape, 0) // 8
    key = lax.broadcasted_iota(jnp.int32, new_scores.shape, 1)
    new_scores = jnp.where(key <= draft, new_scores, -jnp.inf)
    peak = jnp.maximum(
        jnp.max(past_scores, axis=1, keepdims=True), jnp.max(new_scores, axis=1, keepdims=True)
    )
    past_exp = jnp.exp(past_scores - peak)
    new_exp = jnp.exp(new_scores - peak)
    total = jnp.sum(past_exp, axis=1, keepdims=True) + jnp.sum(new_exp, axis=1, keepdims=True)
    past_w = (past_exp / total).astype(jnp.bfloat16)
    new_w = (new_exp / total).astype(jnp.bfloat16)
    mixed = lax.dot_general(past_w, past[:, depth:], nn, preferred_element_type=jnp.float32)
    mixed = mixed + lax.dot_general(new_w, new[:, depth:], nn, preferred_element_type=jnp.float32)
    return mixed.reshape(4, 8, depth).astype(jnp.bfloat16)


def kernel(
    q_in,
    kv_in,
    fresh_in,
    used_in,
    logits_in,
    drafter_in,
    token_in,
    language_in,
    uniform_in,
    attn_out,
    row_out,
    q,
    kv,
    fresh,
    logits,
    drafter,
    used,
    token,
    language,
    uniform,
    tiles,
    shares,
    send,
    arrived,
    terms,
    peaks,
    norms,
    picks,
    stats,
    load_sem,
    send_sem,
    recv_sem,
    stat_send,
    stat_recv,
    ready,
):
    me = lax.axis_index("tensor")
    shift = jnp.where(lax.axis_index("dp") == 0, 1, 0)
    turn = lax.rem(me + (GROUP - 1) * shift, GROUP)

    def rank_at(turn):
        return lax.rem(turn + shift, GROUP)

    def far_first(at):
        near = (at + 1) // 2
        return lax.rem(me + 8 + near * (1 - 2 * ((at + 1) % 2)), GROUP)

    def turn_of(rank):
        return lax.rem(rank + (GROUP - 1) * shift, GROUP)

    barrier = pltpu.get_barrier_semaphore()

    def greet(at, carry):
        peer = rank_at(at)
        pl.semaphore_signal(barrier, inc=1, device_id={"tensor": peer}, device_id_type=MESH)
        return carry

    lax.fori_loop(turn + 1, GROUP, greet, 0)

    loads = []
    for at, (src, dst) in enumerate(
        (
            (logits_in.at[:, :2048], logits.at[:, :2048]),
            (logits_in.at[:, 2048:4096], logits.at[:, 2048:4096]),
            (logits_in.at[:, 4096:6144], logits.at[:, 4096:6144]),
            (logits_in.at[:, 6144:], logits.at[:, 6144:]),
            (language_in, language),
            (drafter_in, drafter),
            (token_in, token),
            (uniform_in, uniform),
            (used_in, used),
            (q_in, q),
            (kv_in, kv),
            (fresh_in, fresh),
        )
    ):
        copy = pltpu.make_async_copy(src, dst, load_sem.at[at])
        if at < 4:
            copy.start()
        loads.append(copy)

    @pl.when(turn > 0)
    def _():
        pl.semaphore_wait(barrier, turn)

    def announce(at, carry):
        peer = far_first(at)

        @pl.when(turn_of(peer) < turn)
        def _():
            pl.semaphore_signal(
                ready.at[me], inc=1, device_id={"tensor": peer}, device_id_type=MESH
            )

        return carry

    lax.fori_loop(0, GROUP - 1, announce, 0)
    for copy in loads[4:]:
        copy.start()

    def logit_tile(at, n):
        if at % 2048 == 0:
            loads[at // 2048].wait()
        return logits[:, at : at + n]

    spread(logit_tile, tiles, ABSENT)

    def pack(slot):
        send[slot] = tiles[pl.ds(slot, CHUNKS, stride=GROUP), :].astype(jnp.bfloat16)


    def block_to(peer):
        return pltpu.make_async_remote_copy(
            src_ref=send.at[peer],
            dst_ref=arrived.at[me],
            send_sem=send_sem.at[peer],
            recv_sem=recv_sem.at[me],
            device_id={"tensor": peer},
            device_id_type=MESH,
        )

    def block_from(peer):
        return pltpu.make_async_remote_copy(
            src_ref=send.at[peer],
            dst_ref=arrived.at[peer],
            send_sem=send_sem.at[peer],
            recv_sem=recv_sem.at[peer],
            device_id={"tensor": peer},
            device_id_type=MESH,
        )

    def send_down(at, carry):
        peer = far_first(at)
        pack(peer)

        @pl.when(turn_of(peer) < turn)
        def _():
            block_to(peer).start()

        return carry

    lax.fori_loop(0, GROUP - 1, send_down, 0)
    arrived[me] = tiles[pl.ds(me, CHUNKS, stride=GROUP), :].astype(jnp.bfloat16)

    def send_up(at, carry):
        peer = rank_at(at)
        pl.semaphore_wait(ready.at[peer], 1)
        block_to(peer).start()
        return carry

    lax.fori_loop(turn + 1, GROUP, send_up, 0)

    for copy in loads[4:]:
        copy.wait()
    lang = language[me // 4]
    spread(lambda at, n: drafter[0, lang, :, at : at + n], tiles, 0.0)
    total = jnp.sum(tiles[...].reshape(CHUNKS * GROUP // 8, 8, LANES), axis=0)
    inverse = 1.0 / jnp.sum(total, axis=(0, 1), keepdims=True)
    place = lax.broadcasted_iota(jnp.int32, (CHUNKS, LANES), 0) * LANES + lax.broadcasted_iota(
        jnp.int32, (CHUNKS, LANES), 1
    )
    wanted = token[me]
    share = jnp.zeros((8, LANES), jnp.float32)
    for p in range(GROUP):
        drafted = tiles[pl.ds(p, CHUNKS, stride=GROUP), :] * inverse
        hit = place == wanted - p * VSHARD
        share = share + jnp.sum(jnp.where(hit, drafted, 0.0).reshape(8, 8, LANES), axis=0)
        shares[p] = drafted.reshape(8, 8, LANES)
    share = jnp.sum(share, axis=(0, 1), keepdims=True)

    for r in range(4):
        attn_out[r] = attend(r, q, kv, fresh, used[r])

    def digest(peer):
        block = arrived[peer].astype(jnp.float32).reshape(8, 8, LANES)
        peak = jnp.max(block, axis=0)
        term = jnp.exp(block - peak[None])
        hit = (place == wanted - peer * VSHARD).reshape(8, 8, LANES)
        peaks[peer] = peak
        terms[peer] = term
        norms[peer] = jnp.sum(term, axis=0)
        picks[peer] = jnp.sum(jnp.where(hit, term, 0.0), axis=0)

    def receive(step, carry):
        at = lax.rem(step + me // 8 * (8 - shift), GROUP)
        peer = rank_at(at)

        @pl.when(at != turn)
        def _():
            block_from(peer).wait_recv()
            digest(peer)

        return carry

    digest(me)
    lax.fori_loop(0, GROUP, receive, 0)

    top = jnp.max(peaks[...], axis=0)
    top = jnp.max(top, axis=(0, 1), keepdims=True)
    scales = jnp.exp(peaks[...] - top[None])
    norm = jnp.sum(norms[...] * scales, axis=0)
    scales = scales * (1.0 / jnp.sum(norm, axis=(0, 1), keepdims=True))[None]
    prob = jnp.sum(picks[...] * scales, axis=0)
    mass = jnp.zeros((8, LANES), jnp.float32)
    for p in range(GROUP):
        mass = mass + jnp.sum(jnp.maximum(terms[p] * scales[p][None] - shares[p], 0.0), axis=0)
    mass = jnp.sum(mass, axis=(0, 1), keepdims=True)
    prob = jnp.sum(prob, axis=(0, 1), keepdims=True)
    margin = jnp.minimum(1.0, prob / share) - uniform[me]

    lane = lax.broadcasted_iota(jnp.int32, (1, LANES), 1)
    row = jnp.where(lane == me, margin, 0.0) + jnp.where(lane == me + GROUP, mass, 0.0)
    stats[me] = row

    def stat_to(peer):
        return pltpu.make_async_remote_copy(
            src_ref=stats.at[me],
            dst_ref=stats.at[me],
            send_sem=stat_send.at[peer],
            recv_sem=stat_recv.at[me],
            device_id={"tensor": peer},
            device_id_type=MESH,
        )

    def stat_start(peer, carry):
        stat_to(peer).start()
        return carry

    lax.fori_loop(0, me, stat_start, 0)
    lax.fori_loop(me + 1, GROUP, stat_start, 0)

    def sent(peer, carry):
        block_to(peer).wait_send()
        return carry

    lax.fori_loop(0, me, sent, 0)
    lax.fori_loop(me + 1, GROUP, sent, 0)

    def stat_done(peer, carry):
        pltpu.make_async_remote_copy(
            src_ref=stats.at[me],
            dst_ref=stats.at[peer],
            send_sem=stat_send.at[peer],
            recv_sem=stat_recv.at[peer],
            device_id={"tensor": peer},
            device_id_type=MESH,
        ).wait()
        return carry

    lax.fori_loop(0, me, stat_done, 0)
    lax.fori_loop(me + 1, GROUP, stat_done, 0)
    row_out[...] = jnp.sum(stats[...], axis=0)


def on_device(
    queries, cache, new_kv, cache_len, target_logits, drafter, draft_tokens, language, uniforms
):
    anywhere = pl.BlockSpec(memory_space=pltpu.HBM)
    vmem = pl.BlockSpec(memory_space=pltpu.VMEM)
    f32 = jnp.float32
    bf16 = jnp.bfloat16
    attn, row = pl.pallas_call(
        kernel,
        out_shape=(
            pltpu.VMEM(queries.shape, bf16),
            pltpu.VMEM((1, LANES), f32),
        ),
        in_specs=[anywhere] * 9,
        out_specs=(vmem, vmem),
        scratch_shapes=[
            pltpu.VMEM(queries.shape, bf16),
            pltpu.VMEM(cache.shape, bf16),
            pltpu.VMEM(new_kv.shape, bf16),
            pltpu.VMEM(target_logits.shape, bf16),
            pltpu.VMEM(drafter.shape, bf16),
            pltpu.SMEM(cache_len.shape, jnp.int32),
            pltpu.SMEM(draft_tokens.shape, jnp.int32),
            pltpu.SMEM(language.shape, jnp.int32),
            pltpu.SMEM(uniforms.shape, f32),
            pltpu.VMEM((CHUNKS * GROUP, LANES), f32),
            pltpu.VMEM((GROUP, 8, 8, LANES), f32),
            pltpu.VMEM((GROUP, CHUNKS, LANES), bf16),
            pltpu.VMEM((GROUP, CHUNKS, LANES), bf16),
            pltpu.VMEM((GROUP, 8, 8, LANES), f32),
            pltpu.VMEM((GROUP, 8, LANES), f32),
            pltpu.VMEM((GROUP, 8, LANES), f32),
            pltpu.VMEM((GROUP, 8, LANES), f32),
            pltpu.VMEM((GROUP, 1, LANES), f32),
            pltpu.SemaphoreType.DMA((12,)),
            pltpu.SemaphoreType.DMA((GROUP,)),
            pltpu.SemaphoreType.DMA((GROUP,)),
            pltpu.SemaphoreType.DMA((GROUP,)),
            pltpu.SemaphoreType.DMA((GROUP,)),
            pltpu.SemaphoreType.REGULAR((GROUP,)),
        ],
        compiler_params=pltpu.CompilerParams(
            collective_id=0, has_side_effects=True, vmem_limit_bytes=60 * 1024 * 1024
        ),
    )(queries, cache, new_kv, cache_len, target_logits, drafter, draft_tokens, language, uniforms)
    return attn, row[0, :GROUP], row[0, GROUP : 2 * GROUP]


def solution(mesh):
    in_specs = (
        P("dp", None, "tensor", None),
        P("tensor", "dp", None, None),
        P("tensor", "dp", None, None),
        P("dp"),
        P("dp", "tensor"),
        P(("dp", "tensor"), None, None, None),
        P("dp"),
        P("dp"),
        P("dp"),
    )
    out_specs = (P("dp", None, "tensor", None), P("dp"), P("dp"))
    return jax.shard_map(
        on_device, mesh=mesh, in_specs=in_specs, out_specs=out_specs, check_vma=False
    )
```

```python
import math

import jax
import jax.numpy as jnp
from jax import lax
from jax.experimental import pallas as pl
from jax.experimental.pallas import tpu as pltpu
from jax.sharding import PartitionSpec as P

MESH = pl.DeviceIdType.MESH
GROUP = 16
LANES = 128
VSHARD = 8016
FULL = VSHARD // LANES
TAIL = VSHARD - FULL * LANES
CHUNKS = 64
ABSENT = -3.0e38


def spread(load, tiles, fill):
    for c in range(FULL):
        tiles[pl.ds(GROUP * c, GROUP), :] = load(c * LANES, LANES).astype(jnp.float32)
    rest = (CHUNKS - FULL) * GROUP
    tiles[pl.ds(GROUP * FULL, rest), :] = jnp.full((rest, LANES), fill, jnp.float32)
    tiles[pl.ds(GROUP * FULL, GROUP), 0:TAIL] = load(FULL * LANES, TAIL).astype(jnp.float32)


def attend(r, q, kv, fresh, used):
    depth = q.shape[-1]
    scale = 1.0 / math.sqrt(depth)
    query = q[r].astype(jnp.float32).reshape(32, depth).astype(jnp.bfloat16)
    nt = (((1,), (1,)), ((), ()))
    nn = (((1,), (0,)), ((), ()))
    past = kv[0, r]
    new = fresh[0, r]
    past_scores = (
        lax.dot_general(query, past[:, :depth], nt, preferred_element_type=jnp.float32) * scale
    )
    new_scores = (
        lax.dot_general(query, new[:, :depth], nt, preferred_element_type=jnp.float32) * scale
    )
    position = lax.broadcasted_iota(jnp.int32, past_scores.shape, 1)
    past_scores = jnp.where(position < used, past_scores, -jnp.inf)
    draft = lax.broadcasted_iota(jnp.int32, new_scores.shape, 0) // 8
    key = lax.broadcasted_iota(jnp.int32, new_scores.shape, 1)
    new_scores = jnp.where(key <= draft, new_scores, -jnp.inf)
    peak = jnp.maximum(
        jnp.max(past_scores, axis=1, keepdims=True), jnp.max(new_scores, axis=1, keepdims=True)
    )
    past_exp = jnp.exp(past_scores - peak)
    new_exp = jnp.exp(new_scores - peak)
    total = jnp.sum(past_exp, axis=1, keepdims=True) + jnp.sum(new_exp, axis=1, keepdims=True)
    past_w = (past_exp / total).astype(jnp.bfloat16)
    new_w = (new_exp / total).astype(jnp.bfloat16)
    mixed = lax.dot_general(past_w, past[:, depth:], nn, preferred_element_type=jnp.float32)
    mixed = mixed + lax.dot_general(new_w, new[:, depth:], nn, preferred_element_type=jnp.float32)
    return mixed.reshape(4, 8, depth).astype(jnp.bfloat16)


def kernel(
    q_in,
    kv_in,
    fresh_in,
    used_in,
    logits_in,
    drafter_in,
    token_in,
    language_in,
    uniform_in,
    attn_out,
    row_out,
    q,
    kv,
    fresh,
    logits,
    drafter,
    used,
    token,
    language,
    uniform,
    tiles,
    shares,
    send,
    arrived,
    terms,
    peaks,
    norms,
    picks,
    stats,
    load_sem,
    send_sem,
    recv_sem,
    stat_send,
    stat_recv,
    ready,
):
    me = lax.axis_index("tensor")
    shift = jnp.where(lax.axis_index("dp") == 0, 1, 0)
    turn = lax.rem(me + (GROUP - 1) * shift, GROUP)

    def rank_at(turn):
        return lax.rem(turn + shift, GROUP)

    def far_first(at):
        near = (at + 1) // 2
        return lax.rem(me + 8 + near * (1 - 2 * ((at + 1) % 2)), GROUP)

    def turn_of(rank):
        return lax.rem(rank + (GROUP - 1) * shift, GROUP)

    barrier = pltpu.get_barrier_semaphore()

    def greet(at, carry):
        peer = rank_at(at)
        pl.semaphore_signal(barrier, inc=1, device_id={"tensor": peer}, device_id_type=MESH)
        return carry

    lax.fori_loop(turn + 1, GROUP, greet, 0)

    loads = []
    for at, (src, dst) in enumerate(
        (
            (logits_in.at[:, :2048], logits.at[:, :2048]),
            (logits_in.at[:, 2048:4096], logits.at[:, 2048:4096]),
            (logits_in.at[:, 4096:6144], logits.at[:, 4096:6144]),
            (logits_in.at[:, 6144:], logits.at[:, 6144:]),
            (language_in, language),
            (drafter_in, drafter),
            (token_in, token),
            (uniform_in, uniform),
            (used_in, used),
            (q_in, q),
            (kv_in, kv),
            (fresh_in, fresh),
        )
    ):
        copy = pltpu.make_async_copy(src, dst, load_sem.at[at])
        if at < 4:
            copy.start()
        loads.append(copy)

    @pl.when(turn > 0)
    def _():
        pl.semaphore_wait(barrier, turn)

    def announce(at, carry):
        peer = far_first(at)

        @pl.when(turn_of(peer) < turn)
        def _():
            pl.semaphore_signal(
                ready.at[me], inc=1, device_id={"tensor": peer}, device_id_type=MESH
            )

        return carry

    lax.fori_loop(0, GROUP - 1, announce, 0)
    for copy in loads[4:]:
        copy.start()

    def logit_tile(at, n):
        if at % 2048 == 0:
            loads[at // 2048].wait()
        return logits[:, at : at + n]

    spread(logit_tile, tiles, ABSENT)

    def pack(slot):
        send[slot] = tiles[pl.ds(slot, CHUNKS, stride=GROUP), :].astype(jnp.bfloat16)


    def block_to(peer):
        return pltpu.make_async_remote_copy(
            src_ref=send.at[peer],
            dst_ref=arrived.at[me],
            send_sem=send_sem.at[peer],
            recv_sem=recv_sem.at[me],
            device_id={"tensor": peer},
            device_id_type=MESH,
        )

    def block_from(peer):
        return pltpu.make_async_remote_copy(
            src_ref=send.at[peer],
            dst_ref=arrived.at[peer],
            send_sem=send_sem.at[peer],
            recv_sem=recv_sem.at[peer],
            device_id={"tensor": peer},
            device_id_type=MESH,
        )

    def send_down(at, carry):
        peer = far_first(at)
        pack(peer)

        @pl.when(turn_of(peer) < turn)
        def _():
            block_to(peer).start()

        return carry

    lax.fori_loop(0, GROUP - 1, send_down, 0)
    arrived[me] = tiles[pl.ds(me, CHUNKS, stride=GROUP), :].astype(jnp.bfloat16)

    def send_up(at, carry):
        peer = rank_at(at)
        pl.semaphore_wait(ready.at[peer], 1)
        block_to(peer).start()
        return carry

    lax.fori_loop(turn + 1, GROUP, send_up, 0)

    for copy in loads[4:]:
        copy.wait()
    lang = language[me // 4]
    spread(lambda at, n: drafter[0, lang, :, at : at + n], tiles, 0.0)
    total = jnp.sum(tiles[...].reshape(CHUNKS * GROUP // 8, 8, LANES), axis=0)
    inverse = 1.0 / jnp.sum(total, axis=(0, 1), keepdims=True)
    place = lax.broadcasted_iota(jnp.int32, (CHUNKS, LANES), 0) * LANES + lax.broadcasted_iota(
        jnp.int32, (CHUNKS, LANES), 1
    )
    wanted = token[me]
    share = jnp.zeros((8, LANES), jnp.float32)
    for p in range(GROUP):
        drafted = tiles[pl.ds(p, CHUNKS, stride=GROUP), :] * inverse
        hit = place == wanted - p * VSHARD
        share = share + jnp.sum(jnp.where(hit, drafted, 0.0).reshape(8, 8, LANES), axis=0)
        shares[p] = drafted.reshape(8, 8, LANES)
    share = jnp.sum(share, axis=(0, 1), keepdims=True)

    for r in range(4):
        attn_out[r] = attend(r, q, kv, fresh, used[r])

    def digest(peer):
        block = arrived[peer].astype(jnp.float32).reshape(8, 8, LANES)
        peak = jnp.max(block, axis=0)
        term = jnp.exp(block - peak[None])
        hit = (place == wanted - peer * VSHARD).reshape(8, 8, LANES)
        peaks[peer] = peak
        terms[peer] = term
        norms[peer] = jnp.sum(term, axis=0)
        picks[peer] = jnp.sum(jnp.where(hit, term, 0.0), axis=0)
        return peak

    first = me // 8 * (8 - shift)

    def receive(step, top):
        at = lax.rem(first + step + jnp.where(step >= turn - first, 1, 0), GROUP)
        peer = rank_at(at)
        block_from(peer).wait_recv()
        return jnp.maximum(top, digest(peer))

    top = lax.fori_loop(0, GROUP - 1, receive, digest(me))
    top = jnp.max(top, axis=(0, 1), keepdims=True)
    scales = jnp.exp(peaks[...] - top[None])
    norm = jnp.sum(norms[...] * scales, axis=0)
    scales = scales * (1.0 / jnp.sum(norm, axis=(0, 1), keepdims=True))[None]
    prob = jnp.sum(picks[...] * scales, axis=0)
    mass = jnp.zeros((8, LANES), jnp.float32)
    for p in range(GROUP):
        mass = mass + jnp.sum(jnp.maximum(terms[p] * scales[p][None] - shares[p], 0.0), axis=0)
    mass = jnp.sum(mass, axis=(0, 1), keepdims=True)
    prob = jnp.sum(prob, axis=(0, 1), keepdims=True)
    margin = jnp.minimum(1.0, prob / share) - uniform[me]

    lane = lax.broadcasted_iota(jnp.int32, (1, LANES), 1)
    row = jnp.where(lane == me, margin, 0.0) + jnp.where(lane == me + GROUP, mass, 0.0)
    stats[me] = row

    def stat_to(peer):
        return pltpu.make_async_remote_copy(
            src_ref=stats.at[me],
            dst_ref=stats.at[me],
            send_sem=stat_send.at[peer],
            recv_sem=stat_recv.at[me],
            device_id={"tensor": peer},
            device_id_type=MESH,
        )

    def stat_start(peer, carry):
        stat_to(peer).start()
        return carry

    lax.fori_loop(0, me, stat_start, 0)
    lax.fori_loop(me + 1, GROUP, stat_start, 0)

    def sent(peer, carry):
        block_to(peer).wait_send()
        return carry

    lax.fori_loop(0, me, sent, 0)
    lax.fori_loop(me + 1, GROUP, sent, 0)

    def stat_done(peer, carry):
        pltpu.make_async_remote_copy(
            src_ref=stats.at[me],
            dst_ref=stats.at[peer],
            send_sem=stat_send.at[peer],
            recv_sem=stat_recv.at[peer],
            device_id={"tensor": peer},
            device_id_type=MESH,
        ).wait()
        return carry

    lax.fori_loop(0, me, stat_done, 0)
    lax.fori_loop(me + 1, GROUP, stat_done, 0)
    row_out[...] = jnp.sum(stats[...], axis=0)


def on_device(
    queries, cache, new_kv, cache_len, target_logits, drafter, draft_tokens, language, uniforms
):
    anywhere = pl.BlockSpec(memory_space=pltpu.HBM)
    vmem = pl.BlockSpec(memory_space=pltpu.VMEM)
    f32 = jnp.float32
    bf16 = jnp.bfloat16
    attn, row = pl.pallas_call(
        kernel,
        out_shape=(
            pltpu.VMEM(queries.shape, bf16),
            pltpu.VMEM((1, LANES), f32),
        ),
        in_specs=[anywhere] * 9,
        out_specs=(vmem, vmem),
        scratch_shapes=[
            pltpu.VMEM(queries.shape, bf16),
            pltpu.VMEM(cache.shape, bf16),
            pltpu.VMEM(new_kv.shape, bf16),
            pltpu.VMEM(target_logits.shape, bf16),
            pltpu.VMEM(drafter.shape, bf16),
            pltpu.SMEM(cache_len.shape, jnp.int32),
            pltpu.SMEM(draft_tokens.shape, jnp.int32),
            pltpu.SMEM(language.shape, jnp.int32),
            pltpu.SMEM(uniforms.shape, f32),
            pltpu.VMEM((CHUNKS * GROUP, LANES), f32),
            pltpu.VMEM((GROUP, 8, 8, LANES), f32),
            pltpu.VMEM((GROUP, CHUNKS, LANES), bf16),
            pltpu.VMEM((GROUP, CHUNKS, LANES), bf16),
            pltpu.VMEM((GROUP, 8, 8, LANES), f32),
            pltpu.VMEM((GROUP, 8, LANES), f32),
            pltpu.VMEM((GROUP, 8, LANES), f32),
            pltpu.VMEM((GROUP, 8, LANES), f32),
            pltpu.VMEM((GROUP, 1, LANES), f32),
            pltpu.SemaphoreType.DMA((12,)),
            pltpu.SemaphoreType.DMA((GROUP,)),
            pltpu.SemaphoreType.DMA((GROUP,)),
            pltpu.SemaphoreType.DMA((GROUP,)),
            pltpu.SemaphoreType.DMA((GROUP,)),
            pltpu.SemaphoreType.REGULAR((GROUP,)),
        ],
        compiler_params=pltpu.CompilerParams(
            collective_id=0, has_side_effects=True, vmem_limit_bytes=60 * 1024 * 1024
        ),
    )(queries, cache, new_kv, cache_len, target_logits, drafter, draft_tokens, language, uniforms)
    return attn, row[0, :GROUP], row[0, GROUP : 2 * GROUP]


def solution(mesh):
    in_specs = (
        P("dp", None, "tensor", None),
        P("tensor", "dp", None, None),
        P("tensor", "dp", None, None),
        P("dp"),
        P("dp", "tensor"),
        P(("dp", "tensor"), None, None, None),
        P("dp"),
        P("dp"),
        P("dp"),
    )
    out_specs = (P("dp", None, "tensor", None), P("dp"), P("dp"))
    return jax.shard_map(
        on_device, mesh=mesh, in_specs=in_specs, out_specs=out_specs, check_vma=False
    )
```

```python
import math

import jax
import jax.numpy as jnp
from jax import lax
from jax.experimental import pallas as pl
from jax.experimental.pallas import tpu as pltpu
from jax.sharding import PartitionSpec as P

MESH = pl.DeviceIdType.MESH
GROUP = 16
LANES = 128
VSHARD = 8016
FULL = VSHARD // LANES
TAIL = VSHARD - FULL * LANES
CHUNKS = 64
ABSENT = -3.0e38


def spread(load, tiles, fill):
    for c in range(FULL):
        tiles[pl.ds(GROUP * c, GROUP), :] = load(c * LANES, LANES).astype(jnp.float32)
    rest = (CHUNKS - FULL) * GROUP
    tiles[pl.ds(GROUP * FULL, rest), :] = jnp.full((rest, LANES), fill, jnp.float32)
    tiles[pl.ds(GROUP * FULL, GROUP), 0:TAIL] = load(FULL * LANES, TAIL).astype(jnp.float32)


def attend(r, q, kv, fresh, used):
    depth = q.shape[-1]
    scale = 1.0 / math.sqrt(depth)
    query = q[r].astype(jnp.float32).reshape(32, depth).astype(jnp.bfloat16)
    nt = (((1,), (1,)), ((), ()))
    nn = (((1,), (0,)), ((), ()))
    past = kv[0, r]
    new = fresh[0, r]
    past_scores = (
        lax.dot_general(query, past[:, :depth], nt, preferred_element_type=jnp.float32) * scale
    )
    new_scores = (
        lax.dot_general(query, new[:, :depth], nt, preferred_element_type=jnp.float32) * scale
    )
    position = lax.broadcasted_iota(jnp.int32, past_scores.shape, 1)
    past_scores = jnp.where(position < used, past_scores, -jnp.inf)
    draft = lax.broadcasted_iota(jnp.int32, new_scores.shape, 0) // 8
    key = lax.broadcasted_iota(jnp.int32, new_scores.shape, 1)
    new_scores = jnp.where(key <= draft, new_scores, -jnp.inf)
    peak = jnp.maximum(
        jnp.max(past_scores, axis=1, keepdims=True), jnp.max(new_scores, axis=1, keepdims=True)
    )
    past_exp = jnp.exp(past_scores - peak)
    new_exp = jnp.exp(new_scores - peak)
    total = jnp.sum(past_exp, axis=1, keepdims=True) + jnp.sum(new_exp, axis=1, keepdims=True)
    past_w = (past_exp / total).astype(jnp.bfloat16)
    new_w = (new_exp / total).astype(jnp.bfloat16)
    mixed = lax.dot_general(past_w, past[:, depth:], nn, preferred_element_type=jnp.float32)
    mixed = mixed + lax.dot_general(new_w, new[:, depth:], nn, preferred_element_type=jnp.float32)
    return mixed.reshape(4, 8, depth).astype(jnp.bfloat16)


def kernel(
    q_in,
    kv_in,
    fresh_in,
    used_in,
    logits_in,
    drafter_in,
    token_in,
    language_in,
    uniform_in,
    attn_out,
    row_out,
    q,
    kv,
    fresh,
    logits,
    drafter,
    used,
    token,
    language,
    uniform,
    tiles,
    shares,
    send,
    arrived,
    terms,
    peaks,
    norms,
    picks,
    stats,
    load_sem,
    send_sem,
    recv_sem,
    stat_send,
    stat_recv,
    ready,
):
    me = lax.axis_index("tensor")
    shift = jnp.where(lax.axis_index("dp") == 0, 1, 0)
    turn = lax.rem(me + (GROUP - 1) * shift, GROUP)

    def rank_at(turn):
        return lax.rem(turn + shift, GROUP)

    def far_first(at):
        near = (at + 1) // 2
        return lax.rem(me + 8 + near * (1 - 2 * ((at + 1) % 2)), GROUP)

    def turn_of(rank):
        return lax.rem(rank + (GROUP - 1) * shift, GROUP)

    barrier = pltpu.get_barrier_semaphore()

    def greet(at, carry):
        peer = rank_at(at)
        pl.semaphore_signal(barrier, inc=1, device_id={"tensor": peer}, device_id_type=MESH)
        return carry

    lax.fori_loop(turn + 1, GROUP, greet, 0)

    loads = []
    for at, (src, dst) in enumerate(
        (
            (logits_in.at[:, :2048], logits.at[:, :2048]),
            (logits_in.at[:, 2048:4096], logits.at[:, 2048:4096]),
            (logits_in.at[:, 4096:6144], logits.at[:, 4096:6144]),
            (logits_in.at[:, 6144:], logits.at[:, 6144:]),
            (language_in, language),
            (drafter_in, drafter),
            (token_in, token),
            (uniform_in, uniform),
            (used_in, used),
            (q_in, q),
            (kv_in, kv),
            (fresh_in, fresh),
        )
    ):
        copy = pltpu.make_async_copy(src, dst, load_sem.at[at])
        if at < 4:
            copy.start()
        loads.append(copy)

    @pl.when(turn > 0)
    def _():
        pl.semaphore_wait(barrier, turn)

    def announce(at, carry):
        peer = far_first(at)

        @pl.when(turn_of(peer) < turn)
        def _():
            pl.semaphore_signal(
                ready.at[me], inc=1, device_id={"tensor": peer}, device_id_type=MESH
            )

        return carry

    lax.fori_loop(0, GROUP - 1, announce, 0)
    for copy in loads[4:]:
        copy.start()

    def logit_tile(at, n):
        if at % 2048 == 0:
            loads[at // 2048].wait()
        return logits[:, at : at + n]

    spread(logit_tile, tiles, ABSENT)

    def pack(slot):
        send[slot] = tiles[pl.ds(slot, CHUNKS, stride=GROUP), :].astype(jnp.bfloat16)


    def block_to(peer):
        return pltpu.make_async_remote_copy(
            src_ref=send.at[peer],
            dst_ref=arrived.at[me],
            send_sem=send_sem.at[peer],
            recv_sem=recv_sem.at[me],
            device_id={"tensor": peer},
            device_id_type=MESH,
        )

    def block_from(peer):
        return pltpu.make_async_remote_copy(
            src_ref=send.at[peer],
            dst_ref=arrived.at[peer],
            send_sem=send_sem.at[peer],
            recv_sem=recv_sem.at[peer],
            device_id={"tensor": peer},
            device_id_type=MESH,
        )

    def send_down(at, carry):
        peer = far_first(at)
        pack(peer)

        @pl.when(turn_of(peer) < turn)
        def _():
            block_to(peer).start()

        return carry

    lax.fori_loop(0, GROUP - 1, send_down, 0)
    arrived[me] = tiles[pl.ds(me, CHUNKS, stride=GROUP), :].astype(jnp.bfloat16)

    def send_up(at, carry):
        at = at + (at // 8) * (4 * ((at % 8) // 4) + 2 * (at % 2) + (at % 4) // 2 - at % 8)
        peer = rank_at(at)

        @pl.when(at > turn)
        def _():
            pl.semaphore_wait(ready.at[peer], 1)
            block_to(peer).start()

        return carry

    lax.fori_loop(0, GROUP, send_up, 0)

    for copy in loads[4:]:
        copy.wait()
    lang = language[me // 4]
    spread(lambda at, n: drafter[0, lang, :, at : at + n], tiles, 0.0)
    total = jnp.sum(tiles[...].reshape(CHUNKS * GROUP // 8, 8, LANES), axis=0)
    inverse = 1.0 / jnp.sum(total, axis=(0, 1), keepdims=True)
    place = lax.broadcasted_iota(jnp.int32, (CHUNKS, LANES), 0) * LANES + lax.broadcasted_iota(
        jnp.int32, (CHUNKS, LANES), 1
    )
    wanted = token[me]
    share = jnp.zeros((8, LANES), jnp.float32)
    for p in range(GROUP):
        drafted = tiles[pl.ds(p, CHUNKS, stride=GROUP), :] * inverse
        hit = place == wanted - p * VSHARD
        share = share + jnp.sum(jnp.where(hit, drafted, 0.0).reshape(8, 8, LANES), axis=0)
        shares[p] = drafted.reshape(8, 8, LANES)
    share = jnp.sum(share, axis=(0, 1), keepdims=True)

    for r in range(4):
        attn_out[r] = attend(r, q, kv, fresh, used[r])

    def digest(peer):
        block = arrived[peer].astype(jnp.float32).reshape(8, 8, LANES)
        peak = jnp.max(block, axis=0)
        term = jnp.exp(block - peak[None])
        hit = (place == wanted - peer * VSHARD).reshape(8, 8, LANES)
        peaks[peer] = peak
        terms[peer] = term
        norms[peer] = jnp.sum(term, axis=0)
        picks[peer] = jnp.sum(jnp.where(hit, term, 0.0), axis=0)
        return peak

    first = me // 8 * (8 - shift)

    def receive(step, top):
        at = lax.rem(first + step + jnp.where(step >= turn - first, 1, 0), GROUP)
        peer = rank_at(at)
        block_from(peer).wait_recv()
        return jnp.maximum(top, digest(peer))

    top = lax.fori_loop(0, GROUP - 1, receive, digest(me))
    top = jnp.max(top, axis=(0, 1), keepdims=True)
    scales = jnp.exp(peaks[...] - top[None])
    norm = jnp.sum(norms[...] * scales, axis=0)
    scales = scales * (1.0 / jnp.sum(norm, axis=(0, 1), keepdims=True))[None]
    prob = jnp.sum(picks[...] * scales, axis=0)
    mass = jnp.zeros((8, LANES), jnp.float32)
    for p in range(GROUP):
        mass = mass + jnp.sum(jnp.maximum(terms[p] * scales[p][None] - shares[p], 0.0), axis=0)
    mass = jnp.sum(mass, axis=(0, 1), keepdims=True)
    prob = jnp.sum(prob, axis=(0, 1), keepdims=True)
    margin = jnp.minimum(1.0, prob / share) - uniform[me]

    lane = lax.broadcasted_iota(jnp.int32, (1, LANES), 1)
    row = jnp.where(lane == me, margin, 0.0) + jnp.where(lane == me + GROUP, mass, 0.0)
    stats[me] = row

    def stat_to(peer):
        return pltpu.make_async_remote_copy(
            src_ref=stats.at[me],
            dst_ref=stats.at[me],
            send_sem=stat_send.at[peer],
            recv_sem=stat_recv.at[me],
            device_id={"tensor": peer},
            device_id_type=MESH,
        )

    def stat_start(peer, carry):
        stat_to(peer).start()
        return carry

    lax.fori_loop(0, me, stat_start, 0)
    lax.fori_loop(me + 1, GROUP, stat_start, 0)

    def sent(peer, carry):
        block_to(peer).wait_send()
        return carry

    lax.fori_loop(0, me, sent, 0)
    lax.fori_loop(me + 1, GROUP, sent, 0)

    def stat_done(peer, carry):
        pltpu.make_async_remote_copy(
            src_ref=stats.at[me],
            dst_ref=stats.at[peer],
            send_sem=stat_send.at[peer],
            recv_sem=stat_recv.at[peer],
            device_id={"tensor": peer},
            device_id_type=MESH,
        ).wait()
        return carry

    lax.fori_loop(0, me, stat_done, 0)
    lax.fori_loop(me + 1, GROUP, stat_done, 0)
    row_out[...] = jnp.sum(stats[...], axis=0)


def on_device(
    queries, cache, new_kv, cache_len, target_logits, drafter, draft_tokens, language, uniforms
):
    anywhere = pl.BlockSpec(memory_space=pltpu.HBM)
    vmem = pl.BlockSpec(memory_space=pltpu.VMEM)
    f32 = jnp.float32
    bf16 = jnp.bfloat16
    attn, row = pl.pallas_call(
        kernel,
        out_shape=(
            pltpu.VMEM(queries.shape, bf16),
            pltpu.VMEM((1, LANES), f32),
        ),
        in_specs=[anywhere] * 9,
        out_specs=(vmem, vmem),
        scratch_shapes=[
            pltpu.VMEM(queries.shape, bf16),
            pltpu.VMEM(cache.shape, bf16),
            pltpu.VMEM(new_kv.shape, bf16),
            pltpu.VMEM(target_logits.shape, bf16),
            pltpu.VMEM(drafter.shape, bf16),
            pltpu.SMEM(cache_len.shape, jnp.int32),
            pltpu.SMEM(draft_tokens.shape, jnp.int32),
            pltpu.SMEM(language.shape, jnp.int32),
            pltpu.SMEM(uniforms.shape, f32),
            pltpu.VMEM((CHUNKS * GROUP, LANES), f32),
            pltpu.VMEM((GROUP, 8, 8, LANES), f32),
            pltpu.VMEM((GROUP, CHUNKS, LANES), bf16),
            pltpu.VMEM((GROUP, CHUNKS, LANES), bf16),
            pltpu.VMEM((GROUP, 8, 8, LANES), f32),
            pltpu.VMEM((GROUP, 8, LANES), f32),
            pltpu.VMEM((GROUP, 8, LANES), f32),
            pltpu.VMEM((GROUP, 8, LANES), f32),
            pltpu.VMEM((GROUP, 1, LANES), f32),
            pltpu.SemaphoreType.DMA((12,)),
            pltpu.SemaphoreType.DMA((GROUP,)),
            pltpu.SemaphoreType.DMA((GROUP,)),
            pltpu.SemaphoreType.DMA((GROUP,)),
            pltpu.SemaphoreType.DMA((GROUP,)),
            pltpu.SemaphoreType.REGULAR((GROUP,)),
        ],
        compiler_params=pltpu.CompilerParams(
            collective_id=0, has_side_effects=True, vmem_limit_bytes=60 * 1024 * 1024
        ),
    )(queries, cache, new_kv, cache_len, target_logits, drafter, draft_tokens, language, uniforms)
    return attn, row[0, :GROUP], row[0, GROUP : 2 * GROUP]


def solution(mesh):
    in_specs = (
        P("dp", None, "tensor", None),
        P("tensor", "dp", None, None),
        P("tensor", "dp", None, None),
        P("dp"),
        P("dp", "tensor"),
        P(("dp", "tensor"), None, None, None),
        P("dp"),
        P("dp"),
        P("dp"),
    )
    out_specs = (P("dp", None, "tensor", None), P("dp"), P("dp"))
    return jax.shard_map(
        on_device, mesh=mesh, in_specs=in_specs, out_specs=out_specs, check_vma=False
    )
```
